512 devices in a mesh: blk: 64 (over y_lo, z, core), uly: 8 (over x, y_hi).
Axes of the slice: x: 4, y: 8 (y_hi: 2, y_lo: 4; y = y_hi * 4 + y_lo), z: 8, core: 2. Of those that a mesh axis runs over, the one named last changes fastest.
Arguments:
- queries: bfloat16 [65536, 2048], P(('blk', 'uly')), may hold values from -6.5 to 6.5
- key_rows: bfloat16 [65536, 256], P(('blk', 'uly')), may hold values from -6.5 to 6.5
- value_rows: bfloat16 [65536, 256], P(('blk', 'uly')), may hold values from -6 to 6
- span_place: int32 [65536], P(('blk', 'uly')), may hold values from 0 to 65535
- span_offset: int32 [65536], P(('blk', 'uly')), may hold values from 0 to 511
- segment_number: int32 [65536], replicated, may hold values from 0 to 4095, never falling along the last dimension, each value on 1 to 32 neighbouring positions
- block_class: int32 [64], replicated, may hold values from 0 to 2
Outputs:
- attended: bfloat16 [65536, 2048], P(('blk', 'uly'))
The draws below stay inside these ranges and needn't reach their ends.
Inputs may be any that keep to these rules, and one draw needn't show every extreme that they name: `segment_number`: segment numbers never fall along the sequence.
All inputs are finite; a program needn't handle non-finite values.
Results may differ from the reference program's by a relative error of at most 0.009.
Values may be sent and summed in bfloat16 or wider, within the bound.
No kernel may reach another device: no remote copies, remote signals or barrier semaphores. Data moves between devices by JAX's collectives and lax.ppermute only.
A program may use at most 64 MiB of HBM per device.

```python
import math
import jax
import jax.numpy as jnp
import numpy as np
from jax import lax

HEADS = 16
HEAD_DIM = 128
KV_GROUPS = 2
SEQ = 65536
NBLK = 64
N_BLK = 64


def draw_queries(key, part):
    key = jax.random.fold_in(key, 11)
    base = jnp.clip(jax.random.normal(key, (SEQ, HEADS, HEAD_DIM), jnp.float32), -6.0, 6.0)
    return base.reshape(SEQ, HEADS * HEAD_DIM).astype(jnp.bfloat16)


def draw_key_rows(key, part):
    key = jax.random.fold_in(key, 23)
    base = jnp.clip(jax.random.normal(key, (SEQ, KV_GROUPS, HEAD_DIM), jnp.float32), -6.0, 6.0)
    return base.reshape(SEQ, KV_GROUPS * HEAD_DIM).astype(jnp.bfloat16)


def plant(array, rng, least, largest):
    longest = array.shape.index(max(array.shape))
    spots = []
    for shift in (0, 1):
        where = [jax.random.randint(jax.random.fold_in(rng, axis), (), 0, length) for axis, length in enumerate(array.shape)]
        where[longest] = (where[longest] + shift) % array.shape[longest]
        spots.append(tuple(where))
    return array.at[spots[0]].set(least).at[spots[1]].set(largest)


def block_scale(own_key, extent, cuts, smallest, high):
    def one(dim, parts):
        heights = jax.random.uniform(jax.random.fold_in(jax.random.fold_in(own_key, 6), dim), (parts,), jnp.float32, smallest / len(cuts), high / len(cuts))
        return jnp.repeat(jnp.exp(heights), extent[dim] // parts).reshape((-1,) + (1,) * (len(extent) - dim - 1))

    gain = one(*cuts[0])
    for cut in cuts[1:]:
        gain = gain * one(*cut)
    return gain


def length_profile(number_of, total, bound, skew):
    loads = [(1 << 20) // math.isqrt(standing ** skew) + 1 for standing in range(2, number_of + 1)]
    spare, given = total - bound - (number_of - 1), [1] * (number_of - 1)
    while spare > 0:
        candidates = [i for i in range(number_of - 1) if given[i] < bound]
        mass, left = sum([loads[i] for i in candidates]), spare
        for i in candidates:
            extra = min(bound - given[i], max(1, left * loads[i] // mass), spare)
            given[i] = given[i] + extra
            spare = spare - extra
    return np.array([bound] + given)


def uneven(rng, number_of, total, most, skew):
    if number_of == 2:
        one = jax.random.randint(rng, (), max(1, total - most), min(most, total - 1) + 1)
        return jnp.stack([one, total - one])
    tallies = jnp.asarray(length_profile(number_of, total, most, skew), jnp.int32)
    couples = (number_of - 1) // 2
    source_of, sink = tallies[1:1 + 2 * couples:2], tallies[2:2 + 2 * couples:2]
    room = jnp.minimum(source_of - 1, most - sink)
    passed = jax.random.randint(jax.random.fold_in(rng, 1), (couples,), 0, 1 << 20) % (room + 1)
    tallies = tallies.at[1:1 + 2 * couples:2].set(source_of - passed).at[2:2 + 2 * couples:2].set(sink + passed)
    return tallies[jax.random.permutation(jax.random.fold_in(rng, 2), number_of)]


def normal_values(stream_key, dims, width, most, cuts=(), kind=jnp.bfloat16):
    values = jax.random.normal(stream_key, dims, jnp.float32) * width
    if len(cuts) > 0:
        values = block_scale(stream_key, dims, cuts, -0.22, 0.18) * values
    return jnp.clip(values, min=-most, max=most).astype(kind)


def setup_inputs(seed: int = 0) -> dict:
    streams_of = jax.random.split(jax.random.key(seed), 8)
    return {
        "queries": draw_queries(jax.random.fold_in(streams_of[7], 71), 0),
        "key_rows": draw_key_rows(jax.random.fold_in(streams_of[7], 71), 0),
        "value_rows": normal_values(streams_of[2], (SEQ, KV_GROUPS * HEAD_DIM), 1.0, 6.0, ((0, 512),)),
        "span_place": plant(jax.random.randint(streams_of[3], (SEQ,), 0, SEQ), jax.random.fold_in(streams_of[3], 1), 0, SEQ - 1).astype(jnp.int32),
        "span_offset": plant(jax.random.randint(streams_of[4], (SEQ,), 0, 512), jax.random.fold_in(streams_of[4], 1), 0, 511).astype(jnp.int32),
        "segment_number": jnp.searchsorted(jnp.cumsum(uneven(streams_of[5], SEQ // 16, SEQ, 32, 1)), jnp.arange(SEQ), side="right").astype(jnp.int32),
        "block_class": plant(jax.random.randint(streams_of[6], (NBLK,), 0, 3), jax.random.fold_in(streams_of[6], 1), 0, 2).astype(jnp.int32),
    }


def rope_pair(part, where):
    half_width = part.shape[-1] // 2
    inverse = 10000.0 ** (-jnp.arange(half_width, dtype=jnp.float32) / half_width)
    angle = where.astype(jnp.float32)[:, None] * inverse[None, :]
    cosine = jnp.cos(angle)[:, None, :]
    sine = jnp.sin(angle)[:, None, :]
    first = part[..., :half_width]
    second = part[..., half_width:]
    return jnp.concatenate([first * cosine - second * sine, second * cosine + first * sine], axis=-1)


def rotary(rows, major, minor):
    count = rows.shape[0]
    heads = rows.reshape(count, -1, HEAD_DIM).astype(jnp.float32)
    quarter = HEAD_DIM // 4
    turned = jnp.concatenate([rope_pair(heads[..., :quarter], major), rope_pair(heads[..., quarter:2 * quarter], minor), heads[..., 2 * quarter:]], axis=-1)
    return turned.reshape(count, -1).astype(jnp.bfloat16)


def visible(klass, query_pos, key_pos, query_ctx, key_ctx, limit):
    valid = (key_pos >= 0) & (key_pos < limit)
    earlier = key_pos[None, :] <= query_pos[:, None]
    infill = key_ctx[None, :] | (jnp.logical_not(query_ctx)[:, None] & earlier)
    rule = jnp.where(klass == 0, True, jnp.where(klass == 1, earlier, infill))
    return valid[None, :] & rule


def softmax_rows(query_block, keys, values, allowed):
    scores = lax.dot_general(query_block, keys, (((1,), (1,)), ((), ())), preferred_element_type=jnp.float32) * (HEAD_DIM ** -0.5)
    scores = jnp.where(allowed, scores, -1e30)
    top = jnp.max(scores, axis=1, keepdims=True)
    expon = jnp.exp(scores - top)
    total = jnp.sum(expon, axis=1, keepdims=True)
    weights = (expon / total).astype(jnp.bfloat16)
    return jnp.dot(weights, values, preferred_element_type=jnp.float32).astype(jnp.bfloat16)


def reference(queries, key_rows, value_rows, span_place, span_offset, segment_number, block_class):
    total = queries.shape[0]
    block = total // N_BLK
    margin = 2 * block
    q_rot = rotary(queries, span_place, span_offset)
    k_rot = rotary(key_rows, span_place, span_offset)
    k_pad = jnp.pad(k_rot, ((margin, margin), (0, 0)))
    v_pad = jnp.pad(value_rows, ((margin, margin), (0, 0)))
    context = segment_number % 2 == 0
    c_pad = jnp.pad(context, (margin, margin))
    per_group = HEADS // KV_GROUPS

    def one_block(index):
        start = index * block
        q_blk = lax.dynamic_slice_in_dim(q_rot, start, block, 0)
        k_win = lax.dynamic_slice_in_dim(k_pad, start, 5 * block, 0)
        v_win = lax.dynamic_slice_in_dim(v_pad, start, 5 * block, 0)
        key_ctx = lax.dynamic_slice_in_dim(c_pad, start, 5 * block, 0)
        query_ctx = lax.dynamic_slice_in_dim(context, start, block, 0)
        query_pos = start + jnp.arange(block, dtype=jnp.int32)
        key_pos = start - margin + jnp.arange(5 * block, dtype=jnp.int32)
        klass = lax.dynamic_index_in_dim(block_class, index, 0, False)
        allowed = visible(klass, query_pos, key_pos, query_ctx, key_ctx, total)

        def one_head(head):
            group = head // per_group
            q_head = lax.dynamic_slice_in_dim(q_blk, head * HEAD_DIM, HEAD_DIM, 1)
            k_head = lax.dynamic_slice_in_dim(k_win, group * HEAD_DIM, HEAD_DIM, 1)
            v_head = lax.dynamic_slice_in_dim(v_win, group * HEAD_DIM, HEAD_DIM, 1)
            return softmax_rows(q_head, k_head, v_head, allowed)

        heads_out = lax.map(one_head, jnp.arange(HEADS, dtype=jnp.int32))
        return jnp.transpose(heads_out, (1, 0, 2)).reshape(block, HEADS * HEAD_DIM)

    result = lax.map(one_block, jnp.arange(N_BLK, dtype=jnp.int32))
    return result.reshape(total, HEADS * HEAD_DIM)
```

```python
import functools

import jax
import jax.numpy as jnp
import numpy as np
from jax import lax
from jax.experimental import pallas as pl
from jax.experimental.pallas import tpu as pltpu
from jax.sharding import PartitionSpec as P

HEAD_DIM = 128
HEADS_PER_GROUP = 8
WIDTH = HEADS_PER_GROUP * HEAD_DIM
ROWS = 128
SHARDS = 8
BLOCK = ROWS * SHARDS
BLOCKS = 64
STACK = 4
NEGATIVE = -1e30
SCALE = HEAD_DIM**-0.5 * 1.4426950408889634
VMEM = pltpu.CompilerParams(vmem_limit_bytes=48 * 2**20)


def lane_frequencies():
    one = 10000.0 ** (-np.arange(16, dtype=np.float64) / 16)
    return np.concatenate([one, one, one, one, np.zeros(64)]).astype(np.float32)[None, :]


def rotate(x, cosine, minus, plus):
    return (
        x * cosine
        + pltpu.roll(x, HEAD_DIM - 16, axis=1) * minus
        + pltpu.roll(x, 16, axis=1) * plus
    )


def keys_kernel(place, offset, frequency, keys, values, payload, tables):
    shape = (ROWS, HEAD_DIM)
    lane = lax.broadcasted_iota(jnp.int32, shape, 1)
    by_place = jnp.broadcast_to(place[...].astype(jnp.float32), shape).T
    by_offset = jnp.broadcast_to(offset[...].astype(jnp.float32), shape).T
    angle = jnp.where(lane < 32, by_place, by_offset) * frequency[...]
    cosine, sine = jnp.cos(angle), jnp.sin(angle)
    first = lane % 32 < 16
    minus = jnp.where(first, -sine, 0.0)
    plus = jnp.where(first, 0.0, sine)
    tables[0], tables[1], tables[2] = cosine, minus, plus
    for group in range(2):
        lanes = slice(group * HEAD_DIM, (group + 1) * HEAD_DIM)
        turned = rotate(keys[:, lanes].astype(jnp.float32), cosine, minus, plus).T.astype(jnp.bfloat16)
        for x in (group, group + 2):
            for half in range(2):
                payload[2 * x + half, :ROWS, :] = turned
                payload[2 * x + half, ROWS:, :] = values[:, lanes]


def queries_kernel(queries, tables, own, other):
    group = lax.axis_index("uly") // 2 % 2
    cosine, minus, plus = tables[0], tables[1], tables[2]
    for out, which in ((other, 1 - group), (own, group)):
        for head in range(HEADS_PER_GROUP):
            start = pl.multiple_of(which * WIDTH + head * HEAD_DIM, HEAD_DIM)
            x = queries[:, pl.ds(start, HEAD_DIM)].astype(jnp.float32)
            out[:, head * HEAD_DIM : (head + 1) * HEAD_DIM] = rotate(x, cosine, minus, plus).astype(jnp.bfloat16)


def attend_kernel(sets, roles, fresh, final, *refs):
    refs = list(refs)
    classes, segments = refs.pop(0), refs.pop(0)
    count = len(sets)
    queries = [refs.pop(0) for _ in range(count)]
    blocks = [refs.pop(0) for _ in roles]
    before = [] if fresh else [(refs.pop(0), refs.pop(0)) for _ in range(count)]
    if final:
        outs = [refs.pop(0) for _ in range(count)]
    else:
        after = [(refs.pop(0), refs.pop(0)) for _ in range(count)]
    split, across, down, total, top, bias = refs

    me, uly = lax.axis_index("blk"), lax.axis_index("uly")
    step = 1 - 2 * (me % 2)
    distance_of = {"own": 0, "near": step, "far": 2 * step, "late": -step, "back": -2 * step}
    klass = classes[me]
    base = jnp.clip(me - 2, 0, BLOCKS - 5)

    for s in range(count):
        for head in range(HEADS_PER_GROUP):
            rows = slice(head * ROWS, (head + 1) * ROWS)
            x = queries[s][:, head * HEAD_DIM : (head + 1) * HEAD_DIM].astype(jnp.float32) * SCALE
            high = x.astype(jnp.bfloat16)
            split[s, rows, :HEAD_DIM] = high
            split[s, rows, HEAD_DIM:] = (x - high.astype(jnp.float32)).astype(jnp.bfloat16)
        if fresh:
            total[s] = jnp.zeros_like(total[s])
            top[s] = jnp.full_like(top[s], NEGATIVE)
        else:
            total[s] = before[s][0][...]
            top[s] = before[s][1][...]
    for j, block in enumerate(blocks):
        down[j, :, HEAD_DIM:] = jnp.ones((BLOCK, HEAD_DIM), jnp.bfloat16)
        for c in range(SHARDS):
            cols = slice(c * ROWS, (c + 1) * ROWS)
            across[j, :HEAD_DIM, cols] = block[c, :ROWS, :]
            across[j, HEAD_DIM:, cols] = block[c, :ROWS, :]
            down[j, cols, :HEAD_DIM] = block[c, ROWS:, :]

    tall = STACK * ROWS
    tiles = HEADS_PER_GROUP // STACK

    def one(s, j, masked):
        def scores(tile):
            return jnp.dot(split[s, tile * tall : (tile + 1) * tall, :], across[j], preferred_element_type=jnp.float32)

        ahead = scores(0)
        for tile in range(tiles):
            now, ahead = ahead, scores(tile + 1) if tile + 1 < tiles else None
            rows = slice(tile * tall, (tile + 1) * tall)
            if masked:
                now = now + jnp.concatenate([bias[...]] * STACK, axis=0)
            old = top[s, rows, :]
            new = jnp.maximum(old, jnp.max(now, axis=1, keepdims=True))
            weights = jnp.exp2(now - jnp.concatenate([new] * SHARDS, axis=1)).astype(jnp.bfloat16)
            part = jnp.dot(weights, down[j], preferred_element_type=jnp.float32)
            decay = jnp.exp2(old - new)
            total[s, rows, :] = total[s, rows, :] * jnp.concatenate([decay, decay], axis=1) + part
            top[s, rows, :] = new

    def block_step(j, carry):
        distance = distance_of[roles[-1]]
        for i in reversed(range(len(roles) - 1)):
            distance = jnp.where(j == i, distance_of[roles[i]], distance)
        there = me + distance
        seen = (there >= 0) & (there < BLOCKS) & ((klass != 1) | (distance <= 0))
        plain = (klass == 0) | ((klass == 1) & (distance < 0))

        @pl.when(seen & plain)
        def _():
            for s in range(count):
                one(s, j, False)

        @pl.when(seen & jnp.logical_not(plain))
        def _():
            row = jnp.clip(there - base, 0, 4)
            key_segment = jnp.concatenate([segments[row * SHARDS + c] for c in range(SHARDS)], axis=1)
            key_context = ((key_segment & 1) == 0) & (klass == 2)
            for s in range(count):
                chunk = uly ^ 2 if sets[s] else uly
                own_segment = segments[(me - base) * SHARDS + chunk]
                odd = jnp.broadcast_to((own_segment & 1).astype(jnp.float32), (ROWS, ROWS)).T
                odd = jnp.where(klass == 1, 1.0, odd)
                causal = jnp.concatenate([odd] * SHARDS, axis=1) > 0.5
                key_at = distance * BLOCK + lax.broadcasted_iota(jnp.int32, (ROWS, BLOCK), 1)
                own_at = chunk * ROWS + lax.broadcasted_iota(jnp.int32, (ROWS, BLOCK), 0)
                allowed = key_context | (causal & (key_at <= own_at))
                bias[...] = jnp.where(allowed, 0.0, NEGATIVE)
                one(s, j, True)

        return carry

    lax.fori_loop(0, len(roles), block_step, 0)
    for s in range(count):
        if final:
            wide = outs[s].shape[1] > WIDTH
            for head in range(HEADS_PER_GROUP):
                state = total[s, head * ROWS : (head + 1) * ROWS, :]
                value = (state[:, :HEAD_DIM] / state[:, HEAD_DIM:]).astype(jnp.bfloat16)
                start = head * HEAD_DIM
                if wide:
                    start = pl.multiple_of(uly // 2 % 2 * WIDTH + start, HEAD_DIM)
                outs[s][:, pl.ds(start, HEAD_DIM)] = value
        else:
            after[s][0][...] = total[s]
            after[s][1][...] = top[s]


def attend(name, classes, segments, sets, queries, blocks, state=None, out=None):
    roles = tuple(blocks)
    count, number = len(sets), len(roles)
    whole = pl.BlockSpec(memory_space=pltpu.VMEM)
    shapes = [
        jax.ShapeDtypeStruct((WIDTH, 2 * HEAD_DIM), jnp.float32),
        jax.ShapeDtypeStruct((WIDTH, HEAD_DIM), jnp.float32),
    ]
    given = [] if state is None else [x for pair in state for x in pair]
    out_shape = shapes * count if out is None else [jax.ShapeDtypeStruct((ROWS, w), jnp.bfloat16) for w in out]
    pairs = count * number * HEADS_PER_GROUP * ROWS * BLOCK
    results = pl.pallas_call(
        functools.partial(attend_kernel, sets, roles, state is None, out is not None),
        out_shape=out_shape,
        in_specs=[pl.BlockSpec(memory_space=pltpu.SMEM)] + [whole] * (1 + count + number + len(given)),
        out_specs=[whole] * len(out_shape),
        scratch_shapes=[
            pltpu.VMEM((count, WIDTH, 2 * HEAD_DIM), jnp.bfloat16),
            pltpu.VMEM((number, 2 * HEAD_DIM, BLOCK), jnp.bfloat16),
            pltpu.VMEM((number, BLOCK, 2 * HEAD_DIM), jnp.bfloat16),
            pltpu.VMEM((count, WIDTH, 2 * HEAD_DIM), jnp.float32),
            pltpu.VMEM((count, WIDTH, HEAD_DIM), jnp.float32),
            pltpu.VMEM((ROWS, BLOCK), jnp.float32),
        ],
        compiler_params=VMEM,
        cost_estimate=pl.CostEstimate(flops=8 * pairs * HEAD_DIM, bytes_accessed=2**20, transcendentals=pairs),
        name=name,
    )(classes, segments, *queries, *blocks.values(), *given)
    if out is not None:
        return results
    return [tuple(results[2 * s : 2 * s + 2]) for s in range(count)]


def shards(queries, key_rows, value_rows, span_place, span_offset, segment_number, block_class):
    me, uly = lax.axis_index("blk"), lax.axis_index("uly")
    payload, tables = pl.pallas_call(
        keys_kernel,
        out_shape=[
            jax.ShapeDtypeStruct((SHARDS, 2 * ROWS, HEAD_DIM), jnp.bfloat16),
            jax.ShapeDtypeStruct((3, ROWS, HEAD_DIM), jnp.float32),
        ],
        compiler_params=VMEM,
        name="rotate_keys",
    )(span_place[None, :], span_offset[None, :], lane_frequencies(), key_rows, value_rows)
    own = lax.all_to_all(payload, "uly", split_axis=0, concat_axis=0, tiled=True)

    q_own, q_other = pl.pallas_call(
        queries_kernel,
        out_shape=[jax.ShapeDtypeStruct((ROWS, WIDTH), jnp.bfloat16)] * 2,
        compiler_params=VMEM,
        name="rotate_queries",
    )(queries, tables)
    partner = [(i, i ^ 2) for i in range(SHARDS)]
    q_partner = lax.ppermute(q_other, "uly", partner)
    first = jnp.clip(me - 2, 0, BLOCKS - 5) * BLOCK
    segments = lax.dynamic_slice(segment_number, (first,), (5 * BLOCK,)).reshape(5 * SHARDS, 1, ROWS)

    within = range(BLOCKS)
    ahead = [(i + 2 - 4 * (i % 2), i) for i in within if i + 2 - 4 * (i % 2) in within]
    behind = [(i - 2 + 4 * (i % 2), i) for i in within if i - 2 + 4 * (i % 2) in within]
    cores = [(i, i ^ 1) for i in within]
    far = lax.ppermute(own, "blk", ahead)
    back = lax.ppermute(own, "blk", behind)
    near, late = lax.ppermute(own, "blk", cores), lax.ppermute(far, "blk", cores)

    run = functools.partial(attend, classes=block_class, segments=segments)
    state = run("attend_own", sets=(True, False), queries=(q_partner, q_own), blocks={"own": own, "near": near})
    (to_send,) = run(
        "attend_partner",
        sets=(True,),
        queries=(q_partner,),
        blocks={"far": far, "late": late, "back": back},
        state=state[:1],
        out=(WIDTH,),
    )
    (mine,) = run(
        "attend_rest",
        sets=(False,),
        queries=(q_own,),
        blocks={"far": far, "late": late, "back": back},
        state=state[1:],
        out=(2 * WIDTH,),
    )
    others = lax.ppermute(to_send, "uly", partner)
    group = uly // 2 % 2
    return lax.dynamic_update_slice(mine, others, (0, (1 - group) * WIDTH))


def solution(mesh):
    rows = P(("blk", "uly"), None)
    line = P(("blk", "uly"))
    return jax.shard_map(
        shards,
        mesh=mesh,
        in_specs=(rows, rows, rows, line, line, P(), P()),
        out_specs=rows,
        check_vma=False,
    )
```

```python
import functools

import jax
import jax.numpy as jnp
import numpy as np
from jax import lax
from jax.experimental import pallas as pl
from jax.experimental.pallas import tpu as pltpu
from jax.sharding import PartitionSpec as P

HEAD_DIM = 128
HEADS_PER_GROUP = 8
WIDTH = HEADS_PER_GROUP * HEAD_DIM
ROWS = 128
SHARDS = 8
BLOCK = ROWS * SHARDS
BLOCKS = 64
STACK = 4
NEGATIVE = -1e30
SCALE = HEAD_DIM**-0.5 * 1.4426950408889634
MAXIMUM = HEAD_DIM + 8
VMEM = pltpu.CompilerParams(vmem_limit_bytes=16 * 2**20)
KEYS_VMEM = 60 * 2**20


def lane_frequencies():
    one = 10000.0 ** (-np.arange(16, dtype=np.float64) / 16)
    return np.concatenate([one, one, one, one, np.zeros(64)]).astype(np.float32)[None, :]


def rotate(x, cosine, minus, plus):
    return (
        x * cosine
        + pltpu.roll(x, HEAD_DIM - 16, axis=1) * minus
        + pltpu.roll(x, 16, axis=1) * plus
    )


def keys_kernel(place_in, offset_in, frequency, keys_in, values_in, payload, tables, place, offset, keys, values, sems):
    copies = [
        pltpu.make_async_copy(source, target, sems.at[i])
        for i, (source, target) in enumerate(
            ((place_in, place), (offset_in, offset), (keys_in, keys), (values_in, values))
        )
    ]
    for copy in copies:
        copy.start()
    copies[0].wait()
    copies[1].wait()
    shape = (ROWS, HEAD_DIM)
    lane = lax.broadcasted_iota(jnp.int32, shape, 1)
    by_place = jnp.broadcast_to(place[...].astype(jnp.float32), shape).T
    by_offset = jnp.broadcast_to(offset[...].astype(jnp.float32), shape).T
    angle = jnp.where(lane < 32, by_place, by_offset) * frequency[...]
    cosine, sine = jnp.cos(angle), jnp.sin(angle)
    first = lane % 32 < 16
    minus = jnp.where(first, -sine, 0.0)
    plus = jnp.where(first, 0.0, sine)
    tables[0], tables[1], tables[2] = cosine, minus, plus
    copies[2].wait()
    copies[3].wait()
    for group in range(2):
        lanes = slice(group * HEAD_DIM, (group + 1) * HEAD_DIM)
        turned = rotate(keys[:, lanes].astype(jnp.float32), cosine, minus, plus).astype(jnp.bfloat16)
        across = values[:, lanes].astype(jnp.float32).T.astype(jnp.bfloat16)
        for x in (group, group + 2):
            for half in range(2):
                payload[2 * x + half, :ROWS, :] = turned
                payload[2 * x + half, ROWS:, :] = across


def split_queries(x, odd, tip):
    x = x * SCALE
    high = x.astype(jnp.bfloat16)
    guard = jnp.where(tip == HEAD_DIM - 1, NEGATIVE, jnp.where(odd > 0.5, 0.0, NEGATIVE))
    low = jnp.where(tip < HEAD_DIM - 2, x - high.astype(jnp.float32), guard)
    return high, low.astype(jnp.bfloat16)


def turn_queries(queries, tables, group, head):
    start = pl.multiple_of(group * WIDTH + head * HEAD_DIM, HEAD_DIM)
    x = queries[:, pl.ds(start, HEAD_DIM)].astype(jnp.float32)
    return rotate(x, tables[0], tables[1], tables[2]).astype(jnp.bfloat16).astype(jnp.float32).T


def other_queries_kernel(queries, tables, other):
    group = 1 - lax.axis_index("uly") // 2 % 2
    for head in range(HEADS_PER_GROUP):
        cols = slice(head * ROWS, (head + 1) * ROWS)
        other[:, cols] = turn_queries(queries, tables, group, head).astype(jnp.bfloat16)


def own_queries_kernel(queries, tables, all_segments, own, odds, segments, sem):
    me, uly = lax.axis_index("blk"), lax.axis_index("uly")
    square = (ROWS, ROWS)
    tip = lax.broadcasted_iota(jnp.int32, square, 0)
    base = jnp.clip(me - 2, 0, BLOCKS - 5)
    copy = pltpu.make_async_copy(all_segments.at[pl.ds(base * SHARDS, 5 * SHARDS)], segments, sem)
    copy.start()
    copy.wait()
    odd = jnp.broadcast_to((segments[(me - base) * SHARDS + uly] & 1).astype(jnp.float32), square)
    for head in range(HEADS_PER_GROUP):
        cols = slice(head * ROWS, (head + 1) * ROWS)
        high, low = split_queries(turn_queries(queries, tables, uly // 2 % 2, head), odd, tip)
        own[:HEAD_DIM, cols] = high
        own[HEAD_DIM:, cols] = low

    def chunk_step(c, carry):
        start = pl.multiple_of(c * ROWS, ROWS)
        column = jnp.broadcast_to((segments[c] & 1).astype(jnp.float32), square).T
        odds[pl.ds(start, ROWS), :] = column.astype(jnp.bfloat16)
        return carry

    lax.fori_loop(0, 5 * SHARDS, chunk_step, 0, unroll=4)


def attend_kernel(sets, roles, pairs, start, final, *refs):
    refs = list(refs)
    classes, segments, odds = refs.pop(0), refs.pop(0), refs.pop(0)
    count = len(sets)
    laid = [(refs.pop(0), refs.pop(0)) for _ in range(pairs)]
    if start:
        arrived = refs.pop(0)
        splits = [None, refs.pop(0)]
    else:
        splits = [refs.pop(0) for _ in range(count)]
    blocks = [] if pairs else [refs.pop(0) for _ in roles]
    given = [] if start else [refs.pop(0) for _ in range(count)]
    states = [refs.pop(0) for _ in range(count)]
    if start:
        splits[0] = refs.pop(0)
    outs = [refs.pop(0) for _ in range(count)] if final else []
    if not pairs:
        laid = [(refs.pop(0), refs.pop(0))]
    (bias,) = refs
    keys = [pair[0].at[i] for pair in laid for i in range(pair[0].shape[0])]
    values = [pair[1].at[i] for pair in laid for i in range(pair[1].shape[0])]

    me, uly = lax.axis_index("blk"), lax.axis_index("uly")
    step = 1 - 2 * (me % 2)
    distance_of = {"own": 0, "near": step, "far": 2 * step, "late": -step, "back": -2 * step}
    klass = classes[me]
    base = jnp.clip(me - 2, 0, BLOCKS - 5)
    square = (ROWS, ROWS)
    lane = lax.broadcasted_iota(jnp.int32, square, 1)
    tip = lax.broadcasted_iota(jnp.int32, square, 0)
    chunks = [uly ^ 2 if theirs else uly for theirs in sets]

    def odd_tokens(s, shape):
        segment = segments[(me - base) * SHARDS + chunks[s]]
        return jnp.broadcast_to((segment & 1).astype(jnp.float32), shape)

    def hidden(s, first, number):
        shape = (number, ROWS)
        at = pl.multiple_of((me - base) * BLOCK + first, ROWS)
        context = (odds[pl.ds(at, number), :].astype(jnp.float32) < 0.5) & (klass == 2)
        follows = (odd_tokens(s, shape) > 0.5) | (klass != 2)
        key_at = first + lax.broadcasted_iota(jnp.int32, shape, 0)
        token_at = chunks[s] * ROWS + lax.broadcasted_iota(jnp.int32, shape, 1)
        return jnp.where(context | (follows & (key_at <= token_at)), 0.0, NEGATIVE)

    facts = []
    for role in roles:
        distance = distance_of[role]
        there = me + distance
        seen = (there >= 0) & (there < BLOCKS) & ((klass != 1) | (distance <= 0))
        facts.append((distance, there, seen))

    def lay_out(j):
        distance, there, _ = facts[j]
        before = jnp.where((klass == 2) & (distance < 0), 1.0, 0.0)
        after = jnp.where((klass == 2) & (distance > 0), 1.0, 0.0)
        guard = jnp.where(lane == HEAD_DIM - 2, before, jnp.where(lane == HEAD_DIM - 1, after, 0.0))
        place = jnp.clip(there - base, 0, 4) * SHARDS
        for c in range(SHARDS):
            rows = slice(c * ROWS, (c + 1) * ROWS)
            part = blocks[j][c, :ROWS, :]
            keys[j][rows, :HEAD_DIM] = part
            odd = odds[pl.ds(pl.multiple_of((place + c) * ROWS, ROWS), ROWS), :].astype(jnp.float32)
            part = jnp.where(lane < HEAD_DIM - 2, part.astype(jnp.float32), odd * guard)
            keys[j][rows, HEAD_DIM:] = part.astype(jnp.bfloat16)
            values[j][:, rows] = blocks[j][c, ROWS:, :]

    wide = STACK * ROWS
    items = [
        (s, slice(tile * wide, (tile + 1) * wide)) for s in range(count) for tile in range(HEADS_PER_GROUP // STACK)
    ]

    def scores(j, s, cols):
        return jnp.dot(keys[j][...], splits[s][:, cols], preferred_element_type=jnp.float32)

    def take(which, masked):
        steps = [(j, s, cols) for j in which for s, cols in items]
        ahead = scores(*steps[0])
        for i, (j, s, cols) in enumerate(steps):
            now, ahead = ahead, scores(*steps[i + 1]) if i + 1 < len(steps) else None
            if masked:
                now = now + jnp.concatenate([bias[s]] * STACK, axis=1)
            weights = jnp.exp2(now - states[s][MAXIMUM : MAXIMUM + 1, cols])
            part = jnp.dot(values[j][...], weights.astype(jnp.bfloat16), preferred_element_type=jnp.float32)
            states[s][:HEAD_DIM, cols] += part
            states[s][HEAD_DIM : HEAD_DIM + 1, cols] += jnp.sum(weights, axis=0, keepdims=True)

    def take_largest(which, masked):
        def head_step(head, carry):
            cols = pl.ds(pl.multiple_of(head * ROWS, ROWS), ROWS)
            for s in range(count):
                now = scores(which[0], s, cols)
                if masked:
                    now = now + bias[s]
                old = states[s][MAXIMUM : MAXIMUM + 1, cols]
                new = jnp.maximum(old, jnp.max(now, axis=0, keepdims=True))
                decay = jnp.exp2(old - new)
                weights = jnp.exp2(now - new)
                part = jnp.dot(values[which[0]][...], weights.astype(jnp.bfloat16), preferred_element_type=jnp.float32)
                states[s][:HEAD_DIM, cols] = states[s][:HEAD_DIM, cols] * decay + part
                total = states[s][HEAD_DIM : HEAD_DIM + 1, cols] * decay + jnp.sum(weights, axis=0, keepdims=True)
                states[s][HEAD_DIM : HEAD_DIM + 1, cols] = total
                states[s][MAXIMUM : MAXIMUM + 1, cols] = new
            return carry

        lax.fori_loop(0, HEADS_PER_GROUP, head_step, 0)

    def each_block(how):
        for j in range(len(roles)):

            @pl.when(facts[j][2])
            def _(j=j):
                how([j], False)

    def own_block(how):
        @pl.when(klass == 0)
        def _():
            how([0], False)

        @pl.when(klass != 0)
        def _():
            how([0], True)

    if start:
        odd = odd_tokens(0, square)
        for head in range(HEADS_PER_GROUP):
            cols = slice(head * ROWS, (head + 1) * ROWS)
            high, low = split_queries(arrived[:, cols].astype(jnp.float32), odd, tip)
            splits[0][:HEAD_DIM, cols] = high
            splits[0][HEAD_DIM:, cols] = low
        lay_out(0)
        for s in range(count):
            rows = pl.ds(pl.multiple_of(chunks[s] * ROWS, ROWS), ROWS)
            near = jnp.dot(keys[0][rows, :], splits[s][...], preferred_element_type=jnp.float32)
            near = near + jnp.concatenate([hidden(s, chunks[s] * ROWS, ROWS)] * HEADS_PER_GROUP, axis=1)
            states[s][:MAXIMUM, :] = jnp.zeros((MAXIMUM, WIDTH), jnp.float32)
            states[s][MAXIMUM : MAXIMUM + 1, :] = jnp.max(near, axis=0, keepdims=True)

        @pl.when(klass != 0)
        def _():
            for s in range(count):
                bias[s] = hidden(s, 0, BLOCK)

        own_block(take)
    else:
        for j in range(len(blocks)):
            lay_out(j)
        for s in range(count):
            states[s][...] = given[s][...]
        every = facts[0][2]
        for fact in facts[1:]:
            every = every & fact[2]

        @pl.when(every)
        def _():
            take(list(range(len(roles))), False)

        @pl.when(jnp.logical_not(every))
        def _():
            each_block(take)

    largest = states[0][HEAD_DIM : HEAD_DIM + 1, :]
    for s in range(1, count):
        largest = jnp.maximum(largest, states[s][HEAD_DIM : HEAD_DIM + 1, :])

    @pl.when(jnp.logical_not(jnp.max(largest) < 2.0**100))
    def _():
        for s in range(count):
            if start:
                states[s][:MAXIMUM, :] = jnp.zeros((MAXIMUM, WIDTH), jnp.float32)
            else:
                states[s][...] = given[s][...]
        if start:
            own_block(take_largest)
        else:
            each_block(take_largest)

    for s, out in enumerate(outs):
        for head in range(HEADS_PER_GROUP):
            cols = slice(head * ROWS, (head + 1) * ROWS)
            value = states[s][:HEAD_DIM, cols] / states[s][HEAD_DIM : HEAD_DIM + 1, cols]
            out[:, cols] = value.T.astype(jnp.bfloat16)


def combine_kernel(mine, others, out, sems):
    group = lax.axis_index("uly") // 2 % 2
    copies = [
        pltpu.make_async_copy(source, out.at[:, pl.ds(pl.multiple_of(which * WIDTH, WIDTH), WIDTH)], sems.at[i])
        for i, (source, which) in enumerate(((mine, group), (others, 1 - group)))
    ]
    for copy in copies:
        copy.start()
    for copy in copies:
        copy.wait()


def attend(name, classes, segments, odds, sets, splits, blocks=None, laid=(), state=None, final=False):
    roles = tuple(blocks) if blocks else tuple(role for group in laid for role in group[0])
    count, number = len(sets), len(roles)
    start = state is None
    whole = pl.BlockSpec(memory_space=pltpu.VMEM)
    shapes = [jax.ShapeDtypeStruct((MAXIMUM + 8, WIDTH), jnp.float32)] * count
    if start:
        shapes.append(jax.ShapeDtypeStruct((2 * HEAD_DIM, WIDTH), jnp.bfloat16))
    if final:
        shapes.append(jax.ShapeDtypeStruct((ROWS, WIDTH), jnp.bfloat16))
    if blocks:
        shapes.append(jax.ShapeDtypeStruct((number, BLOCK, 2 * HEAD_DIM), jnp.bfloat16))
        shapes.append(jax.ShapeDtypeStruct((number, HEAD_DIM, BLOCK), jnp.bfloat16))
    given = [odds, *(x for group in laid for x in group[1:]), *splits, *(blocks or {}).values(), *(state or ())]
    pairs = count * number * HEADS_PER_GROUP * ROWS * BLOCK
    results = list(
        pl.pallas_call(
            functools.partial(attend_kernel, sets, roles, len(laid), start, final),
            out_shape=shapes,
            in_specs=[pl.BlockSpec(memory_space=pltpu.SMEM)] + [whole] * (1 + len(given)),
            out_specs=[whole] * len(shapes),
            scratch_shapes=[pltpu.VMEM((count, BLOCK if start else 8, ROWS), jnp.float32)],
            compiler_params=VMEM,
            cost_estimate=pl.CostEstimate(flops=8 * pairs * HEAD_DIM, bytes_accessed=2**20, transcendentals=pairs),
            name=name,
        )(classes, segments, *given)
    )
    if blocks:
        laid = (roles, *results[-2:])
    states = results[:count]
    if start:
        splits = [results[count], splits[1]]
    return splits, states, laid, results[count] if final else None


def shards(queries, key_rows, value_rows, span_place, span_offset, segment_number, block_class):
    vmem, hbm = pl.BlockSpec(memory_space=pltpu.VMEM), pl.BlockSpec(memory_space=pl.ANY)
    payload, tables = pl.pallas_call(
        keys_kernel,
        out_shape=[
            jax.ShapeDtypeStruct((SHARDS, 2 * ROWS, HEAD_DIM), jnp.bfloat16),
            jax.ShapeDtypeStruct((3, ROWS, HEAD_DIM), jnp.float32),
        ],
        in_specs=[hbm, hbm, vmem, hbm, hbm],
        out_specs=[vmem, vmem],
        scratch_shapes=[
            pltpu.VMEM((1, ROWS), jnp.int32),
            pltpu.VMEM((1, ROWS), jnp.int32),
            pltpu.VMEM((ROWS, 2 * HEAD_DIM), jnp.bfloat16),
            pltpu.VMEM((ROWS, 2 * HEAD_DIM), jnp.bfloat16),
            pltpu.SemaphoreType.DMA((4,)),
        ],
        compiler_params=pltpu.CompilerParams(vmem_limit_bytes=KEYS_VMEM),
        name="rotate_keys",
    )(span_place[None, :], span_offset[None, :], lane_frequencies(), key_rows, value_rows)
    own = lax.all_to_all(payload, "uly", split_axis=0, concat_axis=0, tiled=True)

    q_other = pl.pallas_call(
        other_queries_kernel,
        out_shape=jax.ShapeDtypeStruct((HEAD_DIM, WIDTH), jnp.bfloat16),
        compiler_params=VMEM,
        name="rotate_other_queries",
    )(queries, tables)
    partner = [(i, i ^ 2) for i in range(SHARDS)]
    q_partner = lax.ppermute(q_other, "uly", partner)
    split_own, odds, segments = pl.pallas_call(
        own_queries_kernel,
        out_shape=[
            jax.ShapeDtypeStruct((2 * HEAD_DIM, WIDTH), jnp.bfloat16),
            jax.ShapeDtypeStruct((5 * BLOCK, ROWS), jnp.bfloat16),
            jax.ShapeDtypeStruct((5 * SHARDS, 1, ROWS), jnp.int32),
        ],
        in_specs=[vmem, vmem, hbm],
        out_specs=[vmem, vmem, vmem],
        scratch_shapes=[pltpu.SemaphoreType.DMA],
        compiler_params=VMEM,
        name="rotate_own_queries",
    )(queries, tables, segment_number.reshape(BLOCKS * SHARDS, 1, ROWS))
    ready = (own, split_own, q_partner, odds, segments)
    own, split_own, q_partner, odds, segments = lax.optimization_barrier(ready)

    within = range(BLOCKS)
    ahead = [(i + 2 - 4 * (i % 2), i) for i in within if i + 2 - 4 * (i % 2) in within]
    behind = [(i - 2 + 4 * (i % 2), i) for i in within if i - 2 + 4 * (i % 2) in within]
    cores = [(i, i ^ 1) for i in within]
    far = lax.ppermute(own, "blk", ahead)
    back = lax.ppermute(own, "blk", behind)
    near = lax.ppermute(own, "blk", cores)

    run = functools.partial(attend, classes=block_class, segments=segments, odds=odds)
    both = (True, False)
    splits, state, _, _ = run("attend_own", sets=both, splits=(q_partner, split_own), blocks={"own": own})
    far, state = lax.optimization_barrier((far, state))
    late = lax.ppermute(far, "blk", cores)
    theirs = functools.partial(run, sets=both[:1], splits=splits[:1])
    _, passed, laid, _ = theirs("attend_near", state=state[:1], blocks={"near": near, "far": far})
    _, _, rest, to_send = theirs("attend_partner", state=passed, blocks={"late": late, "back": back}, final=True)
    others = lax.ppermute(to_send, "uly", partner)
    mine = run("attend_rest", sets=both[1:], splits=splits[1:], state=state[1:], laid=(laid, rest), final=True)[3]
    return pl.pallas_call(
        combine_kernel,
        out_shape=jax.ShapeDtypeStruct((ROWS, 2 * WIDTH), jnp.bfloat16),
        in_specs=[vmem, vmem],
        out_specs=hbm,
        scratch_shapes=[pltpu.SemaphoreType.DMA((2,))],
        compiler_params=VMEM,
        name="combine",
    )(mine, others)


def solution(mesh):
    rows = P(("blk", "uly"), None)
    line = P(("blk", "uly"))
    return jax.shard_map(
        shards,
        mesh=mesh,
        in_specs=(rows, rows, rows, line, line, P(), P()),
        out_specs=rows,
        check_vma=False,
    )
```

```python
import functools

import jax
import jax.numpy as jnp
import numpy as np
from jax import lax
from jax.experimental import pallas as pl
from jax.experimental.pallas import tpu as pltpu
from jax.sharding import PartitionSpec as P

HEAD_DIM = 128
HEADS_PER_GROUP = 8
WIDTH = HEADS_PER_GROUP * HEAD_DIM
ROWS = 128
SHARDS = 8
BLOCK = ROWS * SHARDS
BLOCKS = 64
STACK = 8
NEGATIVE = -1e30
SCALE = HEAD_DIM**-0.5 * 1.4426950408889634
MAXIMUM = HEAD_DIM + 8
VMEM = pltpu.CompilerParams(vmem_limit_bytes=16 * 2**20)
KEYS_VMEM = 60 * 2**20


def lane_frequencies():
    one = 10000.0 ** (-np.arange(16, dtype=np.float64) / 16)
    return np.concatenate([one, one, one, one, np.zeros(64)]).astype(np.float32)[None, :]


def partner_of(block, uly):
    return uly ^ (2 + 4 * (block % 2))


def rotate(x, cosine, minus, plus):
    return (
        x * cosine
        + pltpu.roll(x, HEAD_DIM - 16, axis=1) * minus
        + pltpu.roll(x, 16, axis=1) * plus
    )


def keys_kernel(place_in, offset_in, frequency, keys_in, values_in, payload, tables, place, offset, keys, values, sems):
    copies = [
        pltpu.make_async_copy(source, target, sems.at[i])
        for i, (source, target) in enumerate(
            ((place_in, place), (offset_in, offset), (keys_in, keys), (values_in, values))
        )
    ]
    for copy in copies:
        copy.start()
    copies[0].wait()
    copies[1].wait()
    shape = (ROWS, HEAD_DIM)
    lane = lax.broadcasted_iota(jnp.int32, shape, 1)
    by_place = jnp.broadcast_to(place[...].astype(jnp.float32), shape).T
    by_offset = jnp.broadcast_to(offset[...].astype(jnp.float32), shape).T
    angle = jnp.where(lane < 32, by_place, by_offset) * frequency[...]
    cosine, sine = jnp.cos(angle), jnp.sin(angle)
    first = lane % 32 < 16
    minus = jnp.where(first, -sine, 0.0)
    plus = jnp.where(first, 0.0, sine)
    tables[0], tables[1], tables[2] = cosine, minus, plus
    copies[2].wait()
    copies[3].wait()
    for group in range(2):
        lanes = slice(group * HEAD_DIM, (group + 1) * HEAD_DIM)
        turned = rotate(keys[:, lanes].astype(jnp.float32), cosine, minus, plus).astype(jnp.bfloat16)
        across = values[:, lanes].astype(jnp.float32).T.astype(jnp.bfloat16)
        for x in (group, group + 2):
            for half in range(2):
                payload[2 * x + half, :ROWS, :] = turned
                payload[2 * x + half, ROWS:, :] = across


def split_queries(x, odd, tip):
    x = x * SCALE
    high = x.astype(jnp.bfloat16)
    guard = jnp.where(tip == HEAD_DIM - 1, NEGATIVE, jnp.where(odd > 0.5, 0.0, NEGATIVE))
    low = jnp.where(tip < HEAD_DIM - 2, x - high.astype(jnp.float32), guard)
    return high, low.astype(jnp.bfloat16)


def turn_queries(queries, tables, group, head):
    start = pl.multiple_of(group * WIDTH + head * HEAD_DIM, HEAD_DIM)
    x = queries[:, pl.ds(start, HEAD_DIM)].astype(jnp.float32)
    return rotate(x, tables[0], tables[1], tables[2]).astype(jnp.bfloat16).astype(jnp.float32).T


def other_queries_kernel(queries, tables, other):
    group = 1 - lax.axis_index("uly") // 2 % 2
    for head in range(HEADS_PER_GROUP):
        cols = slice(head * ROWS, (head + 1) * ROWS)
        other[:, cols] = turn_queries(queries, tables, group, head).astype(jnp.bfloat16)


def own_queries_kernel(queries, tables, all_segments, own, odds, segments, sem):
    me, uly = lax.axis_index("blk"), lax.axis_index("uly")
    square = (ROWS, ROWS)
    tip = lax.broadcasted_iota(jnp.int32, square, 0)
    base = jnp.clip(me - 2, 0, BLOCKS - 5)
    copy = pltpu.make_async_copy(all_segments.at[pl.ds(base * SHARDS, 5 * SHARDS)], segments, sem)
    copy.start()
    copy.wait()
    odd = jnp.broadcast_to((segments[(me - base) * SHARDS + uly] & 1).astype(jnp.float32), square)
    for head in range(HEADS_PER_GROUP):
        cols = slice(head * ROWS, (head + 1) * ROWS)
        high, low = split_queries(turn_queries(queries, tables, uly // 2 % 2, head), odd, tip)
        own[:HEAD_DIM, cols] = high
        own[HEAD_DIM:, cols] = low

    def chunk_step(c, carry):
        start = pl.multiple_of(c * ROWS, ROWS)
        column = jnp.broadcast_to((segments[c] & 1).astype(jnp.float32), square).T
        odds[pl.ds(start, ROWS), :] = column.astype(jnp.bfloat16)
        return carry

    lax.fori_loop(0, 5 * SHARDS, chunk_step, 0, unroll=4)


def attend_kernel(sets, roles, pairs, start, final, *refs):
    refs = list(refs)
    classes, segments, odds = refs.pop(0), refs.pop(0), refs.pop(0)
    count = len(sets)
    laid = [(refs.pop(0), refs.pop(0)) for _ in range(pairs)]
    if start:
        arrived = refs.pop(0)
        splits = [None, refs.pop(0)]
    else:
        splits = [refs.pop(0) for _ in range(count)]
    blocks = [] if pairs else [refs.pop(0) for _ in roles]
    given = [] if start else [refs.pop(0) for _ in range(count)]
    bias = refs.pop(-1) if start else None
    outs = [refs.pop(0) for _ in range(count)] if final else []
    if final:
        states = refs[-count:]
    else:
        states = [refs.pop(0) for _ in range(count)]
    if start:
        splits[0] = refs.pop(0)
    if not pairs:
        laid = [(refs.pop(0), refs.pop(0))]
    keys = [pair[0].at[i] for pair in laid for i in range(pair[0].shape[0])]
    values = [pair[1].at[i] for pair in laid for i in range(pair[1].shape[0])]

    me, uly = lax.axis_index("blk"), lax.axis_index("uly")
    step = 1 - 2 * (me % 2)
    distance_of = {"own": 0, "near": step, "far": 2 * step, "late": -step, "back": -2 * step}
    klass = classes[me]
    base = jnp.clip(me - 2, 0, BLOCKS - 5)
    square = (ROWS, ROWS)
    lane = lax.broadcasted_iota(jnp.int32, square, 1)
    tip = lax.broadcasted_iota(jnp.int32, square, 0)
    chunks = [partner_of(me, uly) if theirs else uly for theirs in sets]

    def odd_tokens(s, shape):
        segment = segments[(me - base) * SHARDS + chunks[s]]
        return jnp.broadcast_to((segment & 1).astype(jnp.float32), shape)

    def hidden(s, first, number):
        shape = (number, ROWS)
        at = pl.multiple_of((me - base) * BLOCK + first, ROWS)
        context = (odds[pl.ds(at, number), :].astype(jnp.float32) < 0.5) & (klass == 2)
        follows = (odd_tokens(s, shape) > 0.5) | (klass != 2)
        key_at = first + lax.broadcasted_iota(jnp.int32, shape, 0)
        token_at = chunks[s] * ROWS + lax.broadcasted_iota(jnp.int32, shape, 1)
        return jnp.where(context | (follows & (key_at <= token_at)), 0.0, NEGATIVE)

    facts = []
    for role in roles:
        distance = distance_of[role]
        there = me + distance
        seen = (there >= 0) & (there < BLOCKS) & ((klass != 1) | (distance <= 0))
        facts.append((distance, there, seen))

    def lay_out(j):
        distance, there, _ = facts[j]
        before = jnp.where((klass == 2) & (distance < 0), 1.0, 0.0)
        after = jnp.where((klass == 2) & (distance > 0), 1.0, 0.0)
        guard = jnp.where(lane == HEAD_DIM - 2, before, jnp.where(lane == HEAD_DIM - 1, after, 0.0))
        place = jnp.clip(there - base, 0, 4) * SHARDS
        for c in range(SHARDS):
            rows = slice(c * ROWS, (c + 1) * ROWS)
            part = blocks[j][c, :ROWS, :]
            keys[j][rows, :HEAD_DIM] = part
            odd = odds[pl.ds(pl.multiple_of((place + c) * ROWS, ROWS), ROWS), :].astype(jnp.float32)
            part = jnp.where(lane < HEAD_DIM - 2, part.astype(jnp.float32), odd * guard)
            keys[j][rows, HEAD_DIM:] = part.astype(jnp.bfloat16)
            values[j][:, rows] = blocks[j][c, ROWS:, :]

    wide = STACK * ROWS
    items = [
        (s, slice(tile * wide, (tile + 1) * wide)) for s in range(count) for tile in range(HEADS_PER_GROUP // STACK)
    ]

    def scores(j, s, cols):
        return jnp.dot(keys[j][...], splits[s][:, cols], preferred_element_type=jnp.float32)

    def take(which, masked):
        steps = [(j, s, cols) for j in which for s, cols in items]
        tops = [states[s][MAXIMUM : MAXIMUM + 1, :] for s in range(count)]
        ahead = scores(*steps[0])
        for i, (j, s, cols) in enumerate(steps):
            now, ahead = ahead, scores(*steps[i + 1]) if i + 1 < len(steps) else None
            if masked:
                now = now + jnp.concatenate([bias[s]] * STACK, axis=1)
            weights = jnp.exp2(now - tops[s][:, cols])
            part = jnp.dot(values[j][...], weights.astype(jnp.bfloat16), preferred_element_type=jnp.float32)
            states[s][:HEAD_DIM, cols] += part
            states[s][HEAD_DIM : HEAD_DIM + 1, cols] += jnp.sum(weights, axis=0, keepdims=True)

    def take_largest(which, masked):
        def head_step(head, carry):
            cols = pl.ds(pl.multiple_of(head * ROWS, ROWS), ROWS)
            for s in range(count):
                now = scores(which[0], s, cols)
                if masked:
                    now = now + bias[s]
                old = states[s][MAXIMUM : MAXIMUM + 1, cols]
                new = jnp.maximum(old, jnp.max(now, axis=0, keepdims=True))
                decay = jnp.exp2(old - new)
                weights = jnp.exp2(now - new)
                part = jnp.dot(values[which[0]][...], weights.astype(jnp.bfloat16), preferred_element_type=jnp.float32)
                states[s][:HEAD_DIM, cols] = states[s][:HEAD_DIM, cols] * decay + part
                total = states[s][HEAD_DIM : HEAD_DIM + 1, cols] * decay + jnp.sum(weights, axis=0, keepdims=True)
                states[s][HEAD_DIM : HEAD_DIM + 1, cols] = total
                states[s][MAXIMUM : MAXIMUM + 1, cols] = new
            return carry

        lax.fori_loop(0, HEADS_PER_GROUP, head_step, 0)

    def each_block(how):
        for j in range(len(roles)):

            @pl.when(facts[j][2])
            def _(j=j):
                how([j], False)

    def own_block(how):
        @pl.when(klass == 0)
        def _():
            how([0], False)

        @pl.when(klass != 0)
        def _():
            how([0], True)

    if start:
        odd = odd_tokens(0, square)
        for head in range(HEADS_PER_GROUP):
            cols = slice(head * ROWS, (head + 1) * ROWS)
            high, low = split_queries(arrived[:, cols].astype(jnp.float32), odd, tip)
            splits[0][:HEAD_DIM, cols] = high
            splits[0][HEAD_DIM:, cols] = low
        lay_out(0)
        for s in range(count):
            rows = pl.ds(pl.multiple_of(chunks[s] * ROWS, ROWS), ROWS)
            near = jnp.dot(keys[0][rows, :], splits[s][...], preferred_element_type=jnp.float32)
            near = near + jnp.concatenate([hidden(s, chunks[s] * ROWS, ROWS)] * HEADS_PER_GROUP, axis=1)
            states[s][:MAXIMUM, :] = jnp.zeros((MAXIMUM, WIDTH), jnp.float32)
            states[s][MAXIMUM : MAXIMUM + 1, :] = jnp.max(near, axis=0, keepdims=True)

        @pl.when(klass != 0)
        def _():
            for s in range(count):
                bias[s] = hidden(s, 0, BLOCK)

        own_block(take)
    else:
        for j in range(len(blocks)):
            lay_out(j)
        for s in range(count):
            states[s][...] = given[s][...]
        every = facts[0][2]
        for fact in facts[1:]:
            every = every & fact[2]

        @pl.when(every)
        def _():
            take(list(range(len(roles))), False)

        @pl.when(jnp.logical_not(every))
        def _():
            each_block(take)

    largest = states[0][HEAD_DIM : HEAD_DIM + 1, :]
    for s in range(1, count):
        largest = jnp.maximum(largest, states[s][HEAD_DIM : HEAD_DIM + 1, :])

    @pl.when(jnp.logical_not(jnp.max(largest) < 2.0**100))
    def _():
        for s in range(count):
            if start:
                states[s][:MAXIMUM, :] = jnp.zeros((MAXIMUM, WIDTH), jnp.float32)
            else:
                states[s][...] = given[s][...]
        if start:
            own_block(take_largest)
        else:
            each_block(take_largest)

    for s, out in enumerate(outs):
        share = 1.0 / states[s][HEAD_DIM : HEAD_DIM + 1, :]
        for head in range(HEADS_PER_GROUP):
            cols = slice(head * ROWS, (head + 1) * ROWS)
            out[:, cols] = (states[s][:HEAD_DIM, cols] * share[:, cols]).T.astype(jnp.bfloat16)


def combine_kernel(mine, others, out, sems):
    group = lax.axis_index("uly") // 2 % 2
    copies = [
        pltpu.make_async_copy(source, out.at[:, pl.ds(pl.multiple_of(which * WIDTH, WIDTH), WIDTH)], sems.at[i])
        for i, (source, which) in enumerate(((mine, group), (others, 1 - group)))
    ]
    for copy in copies:
        copy.start()
    for copy in copies:
        copy.wait()


def attend(name, classes, segments, odds, sets, splits, blocks=None, laid=(), state=None, keep=True, final=False):
    roles = tuple(blocks) if blocks else tuple(role for group in laid for role in group[0])
    count, number = len(sets), len(roles)
    start = state is None
    whole = pl.BlockSpec(memory_space=pltpu.VMEM)
    state_shape, split_shape = (MAXIMUM + 8, WIDTH), (2 * HEAD_DIM, WIDTH)
    laid_shapes = [(number, BLOCK, 2 * HEAD_DIM), (number, HEAD_DIM, BLOCK)]
    shapes, scratch = [], []
    if final:
        shapes.append(jax.ShapeDtypeStruct((ROWS, WIDTH), jnp.bfloat16))
        laid_out = [jax.ShapeDtypeStruct(shape, jnp.bfloat16) for shape in laid_shapes] if blocks else []
        scratch += [pltpu.VMEM(state_shape, jnp.float32)] * count
    else:
        shapes += [jax.ShapeDtypeStruct(state_shape, jnp.float32)] * count
        laid_out = [jax.ShapeDtypeStruct(shape, jnp.bfloat16) for shape in laid_shapes] if blocks else []
        if start or not keep:
            scratch += [pltpu.VMEM(shape, jnp.bfloat16) for shape in laid_shapes]
            laid_out = []
        if start:
            shapes.append(jax.ShapeDtypeStruct(split_shape, jnp.bfloat16))
            scratch.append(pltpu.VMEM((count, BLOCK, ROWS), jnp.float32))
    shapes += laid_out
    given = [odds, *(x for group in laid for x in group[1:]), *splits, *(blocks or {}).values(), *(state or ())]
    pairs = count * number * HEADS_PER_GROUP * ROWS * BLOCK
    results = list(
        pl.pallas_call(
            functools.partial(attend_kernel, sets, roles, len(laid), start, final),
            out_shape=shapes,
            in_specs=[pl.BlockSpec(memory_space=pltpu.SMEM)] + [whole] * (1 + len(given)),
            out_specs=[whole] * len(shapes),
            scratch_shapes=scratch,
            compiler_params=VMEM,
            cost_estimate=pl.CostEstimate(flops=8 * pairs * HEAD_DIM, bytes_accessed=2**20, transcendentals=pairs),
            name=name,
        )(classes, segments, *given)
    )
    if laid_out:
        laid = (roles, *results[-2:])
    if start:
        splits = [results[count], splits[1]]
    return splits, results[:count], laid, results[0] if final else None


def shards(queries, key_rows, value_rows, span_place, span_offset, segment_number, block_class):
    vmem, hbm = pl.BlockSpec(memory_space=pltpu.VMEM), pl.BlockSpec(memory_space=pl.ANY)
    payload, tables = pl.pallas_call(
        keys_kernel,
        out_shape=[
            jax.ShapeDtypeStruct((SHARDS, 2 * ROWS, HEAD_DIM), jnp.bfloat16),
            jax.ShapeDtypeStruct((3, ROWS, HEAD_DIM), jnp.float32),
        ],
        in_specs=[hbm, hbm, vmem, hbm, hbm],
        out_specs=[vmem, vmem],
        scratch_shapes=[
            pltpu.VMEM((1, ROWS), jnp.int32),
            pltpu.VMEM((1, ROWS), jnp.int32),
            pltpu.VMEM((ROWS, 2 * HEAD_DIM), jnp.bfloat16),
            pltpu.VMEM((ROWS, 2 * HEAD_DIM), jnp.bfloat16),
            pltpu.SemaphoreType.DMA((4,)),
        ],
        compiler_params=pltpu.CompilerParams(vmem_limit_bytes=KEYS_VMEM),
        name="rotate_keys",
    )(span_place[None, :], span_offset[None, :], lane_frequencies(), key_rows, value_rows)
    own = lax.all_to_all(payload, "uly", split_axis=0, concat_axis=0, tiled=True)

    q_other = pl.pallas_call(
        other_queries_kernel,
        out_shape=jax.ShapeDtypeStruct((HEAD_DIM, WIDTH), jnp.bfloat16),
        compiler_params=VMEM,
        name="rotate_other_queries",
    )(queries, tables)
    every = [(b, u) for b in range(BLOCKS) for u in range(SHARDS)]
    partners = [(b * SHARDS + u, b * SHARDS + partner_of(b, u)) for b, u in every]
    q_partner = lax.ppermute(q_other, ("blk", "uly"), partners)
    split_own, odds, segments = pl.pallas_call(
        own_queries_kernel,
        out_shape=[
            jax.ShapeDtypeStruct((2 * HEAD_DIM, WIDTH), jnp.bfloat16),
            jax.ShapeDtypeStruct((5 * BLOCK, ROWS), jnp.bfloat16),
            jax.ShapeDtypeStruct((5 * SHARDS, 1, ROWS), jnp.int32),
        ],
        in_specs=[vmem, vmem, hbm],
        out_specs=[vmem, vmem, vmem],
        scratch_shapes=[pltpu.SemaphoreType.DMA],
        compiler_params=VMEM,
        name="rotate_own_queries",
    )(queries, tables, segment_number.reshape(BLOCKS * SHARDS, 1, ROWS))
    ready = (own, split_own, q_partner, odds, segments)
    own, split_own, q_partner, odds, segments = lax.optimization_barrier(ready)

    within = range(BLOCKS)
    ahead = [(i + 2 - 4 * (i % 2), i) for i in within if i + 2 - 4 * (i % 2) in within]
    behind = [(i - 2 + 4 * (i % 2), i) for i in within if i - 2 + 4 * (i % 2) in within]
    cores = [(i, i ^ 1) for i in within]
    far = lax.ppermute(own, "blk", ahead)
    back = lax.ppermute(own, "blk", behind)
    near = lax.ppermute(own, "blk", cores)

    run = functools.partial(attend, classes=block_class, segments=segments, odds=odds)
    both = (True, False)
    splits, state, _, _ = run("attend_own", sets=both, splits=(q_partner, split_own), blocks={"own": own})
    _, state, _, _ = run("attend_near", sets=both, splits=splits, state=state, blocks={"near": near}, keep=False)
    far, state = lax.optimization_barrier((far, state))
    late = lax.ppermute(far, "blk", cores)
    theirs = functools.partial(run, sets=both[:1], splits=splits[:1])
    _, passed, laid, _ = theirs("attend_far", state=state[:1], blocks={"far": far, "back": back})
    _, _, rest, to_send = theirs("attend_partner", state=passed, blocks={"late": late}, final=True)
    others = lax.ppermute(to_send, ("blk", "uly"), partners)
    mine = run("attend_rest", sets=both[1:], splits=splits[1:], state=state[1:], laid=(laid, rest), final=True)[3]
    return pl.pallas_call(
        combine_kernel,
        out_shape=jax.ShapeDtypeStruct((ROWS, 2 * WIDTH), jnp.bfloat16),
        in_specs=[vmem, vmem],
        out_specs=hbm,
        scratch_shapes=[pltpu.SemaphoreType.DMA((2,))],
        compiler_params=VMEM,
        name="combine",
    )(mine, others)


def solution(mesh):
    rows = P(("blk", "uly"), None)
    line = P(("blk", "uly"))
    return jax.shard_map(
        shards,
        mesh=mesh,
        in_specs=(rows, rows, rows, line, line, P(), P()),
        out_specs=rows,
        check_vma=False,
    )
```

```python
import functools

import jax
import jax.numpy as jnp
import numpy as np
from jax import lax
from jax.experimental import pallas as pl
from jax.experimental.pallas import tpu as pltpu
from jax.sharding import PartitionSpec as P

HEAD_DIM = 128
HEADS_PER_GROUP = 8
WIDTH = HEADS_PER_GROUP * HEAD_DIM
ROWS = 128
SHARDS = 8
BLOCK = ROWS * SHARDS
BLOCKS = 64
STACK = 8
NEGATIVE = -1e30
SCALE = HEAD_DIM**-0.5 * 1.4426950408889634
MAXIMUM = HEAD_DIM + 8
VMEM = pltpu.CompilerParams(vmem_limit_bytes=16 * 2**20)
KEYS_VMEM = 60 * 2**20


def lane_frequencies():
    one = 10000.0 ** (-np.arange(16, dtype=np.float64) / 16)
    return np.concatenate([one, one, one, one, np.zeros(64)]).astype(np.float32)[None, :]


def partner_of(block, uly):
    return uly ^ (2 + 4 * (block % 2))


def rotate(x, cosine, minus, plus):
    return (
        x * cosine
        + pltpu.roll(x, HEAD_DIM - 16, axis=1) * minus
        + pltpu.roll(x, 16, axis=1) * plus
    )


def keys_kernel(*refs):
    place_in, offset_in, frequency, keys_in, values_in, queries_in = refs[:6]
    payload, tables, other, place, offset, keys, values, queries, sems = refs[6:]
    group = 1 - lax.axis_index("uly") // 2 % 2
    queries_in = queries_in.at[:, pl.ds(pl.multiple_of(group * WIDTH, WIDTH), WIDTH)]
    pairs = (place_in, place), (offset_in, offset), (keys_in, keys), (values_in, values), (queries_in, queries)
    copies = [pltpu.make_async_copy(source, target, sems.at[i]) for i, (source, target) in enumerate(pairs)]
    for copy in copies:
        copy.start()
    copies[0].wait()
    copies[1].wait()
    shape = (ROWS, HEAD_DIM)
    lane = lax.broadcasted_iota(jnp.int32, shape, 1)
    by_place = jnp.broadcast_to(place[...].astype(jnp.float32), shape).T
    by_offset = jnp.broadcast_to(offset[...].astype(jnp.float32), shape).T
    angle = jnp.where(lane < 32, by_place, by_offset) * frequency[...]
    cosine, sine = jnp.cos(angle), jnp.sin(angle)
    first = lane % 32 < 16
    minus = jnp.where(first, -sine, 0.0)
    plus = jnp.where(first, 0.0, sine)
    tables[0], tables[1], tables[2] = cosine, minus, plus
    copies[2].wait()
    copies[3].wait()
    for group in range(2):
        lanes = slice(group * HEAD_DIM, (group + 1) * HEAD_DIM)
        turned = rotate(keys[:, lanes].astype(jnp.float32), cosine, minus, plus).astype(jnp.bfloat16)
        across = values[:, lanes].astype(jnp.float32).T.astype(jnp.bfloat16)
        for x in (group, group + 2):
            for half in range(2):
                payload[2 * x + half, :ROWS, :] = turned
                payload[2 * x + half, ROWS:, :] = across
    copies[4].wait()
    for head in range(HEADS_PER_GROUP):
        cols = slice(head * ROWS, (head + 1) * ROWS)
        turned = rotate(queries[:, cols].astype(jnp.float32), cosine, minus, plus).astype(jnp.bfloat16)
        other[:, cols] = turned.astype(jnp.float32).T.astype(jnp.bfloat16)


def split_queries(x, odd, tip):
    x = x * SCALE
    high = x.astype(jnp.bfloat16)
    guard = jnp.where(tip == HEAD_DIM - 1, NEGATIVE, jnp.where(odd > 0.5, 0.0, NEGATIVE))
    low = jnp.where(tip < HEAD_DIM - 2, x - high.astype(jnp.float32), guard)
    return high, low.astype(jnp.bfloat16)


def turn_queries(queries, tables, group, head):
    start = pl.multiple_of(group * WIDTH + head * HEAD_DIM, HEAD_DIM)
    x = queries[:, pl.ds(start, HEAD_DIM)].astype(jnp.float32)
    return rotate(x, tables[0], tables[1], tables[2]).astype(jnp.bfloat16).astype(jnp.float32).T


def own_queries_kernel(queries, tables, all_segments, own, odds, segments, sem):
    me, uly = lax.axis_index("blk"), lax.axis_index("uly")
    square = (ROWS, ROWS)
    tip = lax.broadcasted_iota(jnp.int32, square, 0)
    base = jnp.clip(me - 2, 0, BLOCKS - 5)
    copy = pltpu.make_async_copy(all_segments.at[pl.ds(base * SHARDS, 5 * SHARDS)], segments, sem)
    copy.start()
    copy.wait()
    odd = jnp.broadcast_to((segments[(me - base) * SHARDS + uly] & 1).astype(jnp.float32), square)
    for head in range(HEADS_PER_GROUP):
        cols = slice(head * ROWS, (head + 1) * ROWS)
        high, low = split_queries(turn_queries(queries, tables, uly // 2 % 2, head), odd, tip)
        own[:HEAD_DIM, cols] = high
        own[HEAD_DIM:, cols] = low

    def chunk_step(c, carry):
        start = pl.multiple_of(c * ROWS, ROWS)
        column = jnp.broadcast_to((segments[c] & 1).astype(jnp.float32), square).T
        odds[pl.ds(start, ROWS), :] = column.astype(jnp.bfloat16)
        return carry

    lax.fori_loop(0, 5 * SHARDS, chunk_step, 0, unroll=4)


def attend_kernel(sets, roles, pairs, start, final, *refs):
    refs = list(refs)
    classes, segments, odds = refs.pop(0), refs.pop(0), refs.pop(0)
    count = len(sets)
    laid = [(refs.pop(0), refs.pop(0)) for _ in range(pairs)]
    if start:
        arrived = refs.pop(0)
        splits = [None, refs.pop(0)]
    else:
        splits = [refs.pop(0) for _ in range(count)]
    blocks = [] if pairs else [refs.pop(0) for _ in roles]
    given = [] if start else [refs.pop(0) for _ in range(count)]
    bias = refs.pop(-1) if start else None
    outs = [refs.pop(0) for _ in range(count)] if final else []
    if final:
        states = refs[-count:]
    else:
        states = [refs.pop(0) for _ in range(count)]
    if start:
        splits[0] = refs.pop(0)
    if not pairs:
        laid = [(refs.pop(0), refs.pop(0))]
    keys = [pair[0].at[i] for pair in laid for i in range(pair[0].shape[0])]
    values = [pair[1].at[i] for pair in laid for i in range(pair[1].shape[0])]

    me, uly = lax.axis_index("blk"), lax.axis_index("uly")
    step = 1 - 2 * (me % 2)
    distance_of = {"own": 0, "near": step, "far": 2 * step, "late": -step, "back": -2 * step}
    klass = classes[me]
    base = jnp.clip(me - 2, 0, BLOCKS - 5)
    square = (ROWS, ROWS)
    lane = lax.broadcasted_iota(jnp.int32, square, 1)
    tip = lax.broadcasted_iota(jnp.int32, square, 0)
    chunks = [partner_of(me, uly) if theirs else uly for theirs in sets]

    def odd_tokens(s, shape):
        segment = segments[(me - base) * SHARDS + chunks[s]]
        return jnp.broadcast_to((segment & 1).astype(jnp.float32), shape)

    def hidden(s, first, number):
        shape = (number, ROWS)
        at = pl.multiple_of((me - base) * BLOCK + first, ROWS)
        context = (odds[pl.ds(at, number), :].astype(jnp.float32) < 0.5) & (klass == 2)
        follows = (odd_tokens(s, shape) > 0.5) | (klass != 2)
        key_at = first + lax.broadcasted_iota(jnp.int32, shape, 0)
        token_at = chunks[s] * ROWS + lax.broadcasted_iota(jnp.int32, shape, 1)
        return jnp.where(context | (follows & (key_at <= token_at)), 0.0, NEGATIVE)

    facts = []
    for role in roles:
        distance = distance_of[role]
        there = me + distance
        seen = (there >= 0) & (there < BLOCKS) & ((klass != 1) | (distance <= 0))
        facts.append((distance, there, seen))

    def lay_out(j):
        distance, there, _ = facts[j]
        before = jnp.where((klass == 2) & (distance < 0), 1.0, 0.0)
        after = jnp.where((klass == 2) & (distance > 0), 1.0, 0.0)
        guard = jnp.where(lane == HEAD_DIM - 2, before, jnp.where(lane == HEAD_DIM - 1, after, 0.0))
        place = jnp.clip(there - base, 0, 4) * SHARDS
        for c in range(SHARDS):
            rows = slice(c * ROWS, (c + 1) * ROWS)
            part = blocks[j][c, :ROWS, :]
            keys[j][rows, :HEAD_DIM] = part
            odd = odds[pl.ds(pl.multiple_of((place + c) * ROWS, ROWS), ROWS), :].astype(jnp.float32)
            part = jnp.where(lane < HEAD_DIM - 2, part.astype(jnp.float32), odd * guard)
            keys[j][rows, HEAD_DIM:] = part.astype(jnp.bfloat16)
            values[j][:, rows] = blocks[j][c, ROWS:, :]

    wide = STACK * ROWS
    items = [
        (s, slice(tile * wide, (tile + 1) * wide)) for s in range(count) for tile in range(HEADS_PER_GROUP // STACK)
    ]

    def scores(j, s, cols):
        return jnp.dot(keys[j][...], splits[s][:, cols], preferred_element_type=jnp.float32)

    def take(which, masked):
        steps = [(j, s, cols) for j in which for s, cols in items]
        tops = [states[s][MAXIMUM : MAXIMUM + 1, :] for s in range(count)]
        ahead = scores(*steps[0])
        for i, (j, s, cols) in enumerate(steps):
            now, ahead = ahead, scores(*steps[i + 1]) if i + 1 < len(steps) else None
            if masked:
                now = now + jnp.concatenate([bias[s]] * STACK, axis=1)
            weights = jnp.exp2(now - tops[s][:, cols])
            part = jnp.dot(values[j][...], weights.astype(jnp.bfloat16), preferred_element_type=jnp.float32)
            states[s][:HEAD_DIM, cols] += part
            states[s][HEAD_DIM : HEAD_DIM + 1, cols] += jnp.sum(weights, axis=0, keepdims=True)

    def take_largest(which, masked):
        def head_step(head, carry):
            cols = pl.ds(pl.multiple_of(head * ROWS, ROWS), ROWS)
            for s in range(count):
                now = scores(which[0], s, cols)
                if masked:
                    now = now + bias[s]
                old = states[s][MAXIMUM : MAXIMUM + 1, cols]
                new = jnp.maximum(old, jnp.max(now, axis=0, keepdims=True))
                decay = jnp.exp2(old - new)
                weights = jnp.exp2(now - new)
                part = jnp.dot(values[which[0]][...], weights.astype(jnp.bfloat16), preferred_element_type=jnp.float32)
                states[s][:HEAD_DIM, cols] = states[s][:HEAD_DIM, cols] * decay + part
                total = states[s][HEAD_DIM : HEAD_DIM + 1, cols] * decay + jnp.sum(weights, axis=0, keepdims=True)
                states[s][HEAD_DIM : HEAD_DIM + 1, cols] = total
                states[s][MAXIMUM : MAXIMUM + 1, cols] = new
            return carry

        lax.fori_loop(0, HEADS_PER_GROUP, head_step, 0)

    def each_block(how):
        for j in range(len(roles)):

            @pl.when(facts[j][2])
            def _(j=j):
                how([j], False)

    def own_block(how):
        @pl.when(klass == 0)
        def _():
            how([0], False)

        @pl.when(klass != 0)
        def _():
            how([0], True)

    if start:
        odd = odd_tokens(0, square)
        for head in range(HEADS_PER_GROUP):
            cols = slice(head * ROWS, (head + 1) * ROWS)
            high, low = split_queries(arrived[:, cols].astype(jnp.float32), odd, tip)
            splits[0][:HEAD_DIM, cols] = high
            splits[0][HEAD_DIM:, cols] = low
        lay_out(0)
        for s in range(count):
            rows = pl.ds(pl.multiple_of(chunks[s] * ROWS, ROWS), ROWS)
            near = jnp.dot(keys[0][rows, :], splits[s][...], preferred_element_type=jnp.float32)
            near = near + jnp.concatenate([hidden(s, chunks[s] * ROWS, ROWS)] * HEADS_PER_GROUP, axis=1)
            states[s][:MAXIMUM, :] = jnp.zeros((MAXIMUM, WIDTH), jnp.float32)
            states[s][MAXIMUM : MAXIMUM + 1, :] = jnp.max(near, axis=0, keepdims=True)

        @pl.when(klass != 0)
        def _():
            for s in range(count):
                bias[s] = hidden(s, 0, BLOCK)

        own_block(take)
    else:
        for j in range(len(blocks)):
            lay_out(j)
        for s in range(count):
            states[s][...] = given[s][...]
        every = facts[0][2]
        for fact in facts[1:]:
            every = every & fact[2]

        @pl.when(every)
        def _():
            take(list(range(len(roles))), False)

        @pl.when(jnp.logical_not(every))
        def _():
            each_block(take)

    largest = states[0][HEAD_DIM : HEAD_DIM + 1, :]
    for s in range(1, count):
        largest = jnp.maximum(largest, states[s][HEAD_DIM : HEAD_DIM + 1, :])

    @pl.when(jnp.logical_not(jnp.max(largest) < 2.0**100))
    def _():
        for s in range(count):
            if start:
                states[s][:MAXIMUM, :] = jnp.zeros((MAXIMUM, WIDTH), jnp.float32)
            else:
                states[s][...] = given[s][...]
        if start:
            own_block(take_largest)
        else:
            each_block(take_largest)

    for s, out in enumerate(outs):
        share = 1.0 / states[s][HEAD_DIM : HEAD_DIM + 1, :]
        for head in range(HEADS_PER_GROUP):
            cols = slice(head * ROWS, (head + 1) * ROWS)
            out[:, cols] = (states[s][:HEAD_DIM, cols] * share[:, cols]).T.astype(jnp.bfloat16)


def combine_kernel(mine, others, out, sems):
    group = lax.axis_index("uly") // 2 % 2
    copies = [
        pltpu.make_async_copy(source, out.at[:, pl.ds(pl.multiple_of(which * WIDTH, WIDTH), WIDTH)], sems.at[i])
        for i, (source, which) in enumerate(((mine, group), (others, 1 - group)))
    ]
    for copy in copies:
        copy.start()
    for copy in copies:
        copy.wait()


def attend(name, classes, segments, odds, sets, splits, blocks=None, laid=(), state=None, final=False):
    roles = tuple(blocks) if blocks else tuple(role for group in laid for role in group[0])
    count, number = len(sets), len(roles)
    start = state is None
    whole = pl.BlockSpec(memory_space=pltpu.VMEM)
    state_shape, split_shape = (MAXIMUM + 8, WIDTH), (2 * HEAD_DIM, WIDTH)
    laid_shapes = [(number, BLOCK, 2 * HEAD_DIM), (number, HEAD_DIM, BLOCK)]
    shapes, scratch = [], []
    if final:
        shapes.append(jax.ShapeDtypeStruct((ROWS, WIDTH), jnp.bfloat16))
        laid_out = [jax.ShapeDtypeStruct(shape, jnp.bfloat16) for shape in laid_shapes] if blocks else []
        scratch += [pltpu.VMEM(state_shape, jnp.float32)] * count
    else:
        shapes += [jax.ShapeDtypeStruct(state_shape, jnp.float32)] * count
        laid_out = [jax.ShapeDtypeStruct(shape, jnp.bfloat16) for shape in laid_shapes] if blocks else []
        if start:
            scratch += [pltpu.VMEM(shape, jnp.bfloat16) for shape in laid_shapes]
            laid_out = []
            shapes.append(jax.ShapeDtypeStruct(split_shape, jnp.bfloat16))
            scratch.append(pltpu.VMEM((count, BLOCK, ROWS), jnp.float32))
    shapes += laid_out
    given = [odds, *(x for group in laid for x in group[1:]), *splits, *(blocks or {}).values(), *(state or ())]
    pairs = count * number * HEADS_PER_GROUP * ROWS * BLOCK
    results = list(
        pl.pallas_call(
            functools.partial(attend_kernel, sets, roles, len(laid), start, final),
            out_shape=shapes,
            in_specs=[pl.BlockSpec(memory_space=pltpu.SMEM)] + [whole] * (1 + len(given)),
            out_specs=[whole] * len(shapes),
            scratch_shapes=scratch,
            compiler_params=VMEM,
            cost_estimate=pl.CostEstimate(flops=8 * pairs * HEAD_DIM, bytes_accessed=2**20, transcendentals=pairs),
            name=name,
        )(classes, segments, *given)
    )
    if laid_out:
        laid = (roles, *results[-2:])
    if start:
        splits = [results[count], splits[1]]
    return splits, results[:count], laid, results[0] if final else None


def shards(queries, key_rows, value_rows, span_place, span_offset, segment_number, block_class):
    vmem, hbm = pl.BlockSpec(memory_space=pltpu.VMEM), pl.BlockSpec(memory_space=pl.ANY)
    payload, tables, q_other = pl.pallas_call(
        keys_kernel,
        out_shape=[
            jax.ShapeDtypeStruct((SHARDS, 2 * ROWS, HEAD_DIM), jnp.bfloat16),
            jax.ShapeDtypeStruct((3, ROWS, HEAD_DIM), jnp.float32),
            jax.ShapeDtypeStruct((HEAD_DIM, WIDTH), jnp.bfloat16),
        ],
        in_specs=[hbm, hbm, vmem, hbm, hbm, hbm],
        out_specs=[vmem, vmem, vmem],
        scratch_shapes=[
            pltpu.VMEM((1, ROWS), jnp.int32),
            pltpu.VMEM((1, ROWS), jnp.int32),
            pltpu.VMEM((ROWS, 2 * HEAD_DIM), jnp.bfloat16),
            pltpu.VMEM((ROWS, 2 * HEAD_DIM), jnp.bfloat16),
            pltpu.VMEM((ROWS, WIDTH), jnp.bfloat16),
            pltpu.SemaphoreType.DMA((5,)),
        ],
        compiler_params=pltpu.CompilerParams(vmem_limit_bytes=KEYS_VMEM),
        name="rotate_keys",
    )(span_place[None, :], span_offset[None, :], lane_frequencies(), key_rows, value_rows, queries)
    own = lax.all_to_all(payload, "uly", split_axis=0, concat_axis=0, tiled=True)

    every = [(b, u) for b in range(BLOCKS) for u in range(SHARDS)]
    partners = [(b * SHARDS + u, b * SHARDS + partner_of(b, u)) for b, u in every]
    q_partner = lax.ppermute(q_other, ("blk", "uly"), partners)
    split_own, odds, segments = pl.pallas_call(
        own_queries_kernel,
        out_shape=[
            jax.ShapeDtypeStruct((2 * HEAD_DIM, WIDTH), jnp.bfloat16),
            jax.ShapeDtypeStruct((5 * BLOCK, ROWS), jnp.bfloat16),
            jax.ShapeDtypeStruct((5 * SHARDS, 1, ROWS), jnp.int32),
        ],
        in_specs=[vmem, vmem, hbm],
        out_specs=[vmem, vmem, vmem],
        scratch_shapes=[pltpu.SemaphoreType.DMA],
        compiler_params=VMEM,
        name="rotate_own_queries",
    )(queries, tables, segment_number.reshape(BLOCKS * SHARDS, 1, ROWS))
    ready = (own, split_own, q_partner, odds, segments)
    own, split_own, q_partner, odds, segments = lax.optimization_barrier(ready)

    within = range(BLOCKS)
    ahead = [(i + 2 - 4 * (i % 2), i) for i in within if i + 2 - 4 * (i % 2) in within]
    behind = [(i - 2 + 4 * (i % 2), i) for i in within if i - 2 + 4 * (i % 2) in within]
    cores = [(i, i ^ 1) for i in within]
    far = lax.ppermute(own, "blk", ahead)
    back = lax.ppermute(own, "blk", behind)
    near = lax.ppermute(own, "blk", cores)

    run = functools.partial(attend, classes=block_class, segments=segments, odds=odds)
    both = (True, False)
    splits, state, _, _ = run("attend_own", sets=both, splits=(q_partner, split_own), blocks={"own": own})
    far, state = lax.optimization_barrier((far, state))
    late = lax.ppermute(far, "blk", cores)
    theirs = functools.partial(run, sets=both[:1], splits=splits[:1])
    _, passed, laid, _ = theirs("attend_near", state=state[:1], blocks={"near": near, "far": far})
    _, _, rest, to_send = theirs("attend_partner", state=passed, blocks={"late": late, "back": back}, final=True)
    others = lax.ppermute(to_send, ("blk", "uly"), partners)
    mine = run("attend_rest", sets=both[1:], splits=splits[1:], state=state[1:], laid=(laid, rest), final=True)[3]
    return pl.pallas_call(
        combine_kernel,
        out_shape=jax.ShapeDtypeStruct((ROWS, 2 * WIDTH), jnp.bfloat16),
        in_specs=[vmem, vmem],
        out_specs=hbm,
        scratch_shapes=[pltpu.SemaphoreType.DMA((2,))],
        compiler_params=VMEM,
        name="combine",
    )(mine, others)


def solution(mesh):
    rows = P(("blk", "uly"), None)
    line = P(("blk", "uly"))
    return jax.shard_map(
        shards,
        mesh=mesh,
        in_specs=(rows, rows, rows, line, line, P(), P()),
        out_specs=rows,
        check_vma=False,
    )
```

```python
import functools

import jax
import jax.numpy as jnp
import numpy as np
from jax import lax
from jax.experimental import pallas as pl
from jax.experimental.pallas import tpu as pltpu
from jax.sharding import PartitionSpec as P

HEAD_DIM = 128
HEADS_PER_GROUP = 8
WIDTH = HEADS_PER_GROUP * HEAD_DIM
ROWS = 128
SHARDS = 8
BLOCK = ROWS * SHARDS
BLOCKS = 64
STACK = 8
NEGATIVE = -1e30
SCALE = HEAD_DIM**-0.5 * 1.4426950408889634
MAXIMUM = HEAD_DIM + 8
VMEM = pltpu.CompilerParams(vmem_limit_bytes=16 * 2**20)
KEYS_VMEM = 60 * 2**20


def lane_frequencies():
    one = 10000.0 ** (-np.arange(16, dtype=np.float64) / 16)
    return np.concatenate([one, one, one, one, np.zeros(64)]).astype(np.float32)[None, :]


def partner_of(block, uly):
    return uly ^ (2 + 4 * (block % 2))


def rotate(x, cosine, minus, plus):
    return (
        x * cosine
        + pltpu.roll(x, HEAD_DIM - 16, axis=1) * minus
        + pltpu.roll(x, 16, axis=1) * plus
    )


def keys_kernel(*refs):
    place_in, offset_in, frequency, keys_in, values_in, queries_in = refs[:6]
    payload, tables, other, place, offset, keys, values, queries, sems = refs[6:]
    group = 1 - lax.axis_index("uly") // 2 % 2
    queries_in = queries_in.at[:, pl.ds(pl.multiple_of(group * WIDTH, WIDTH), WIDTH)]
    pairs = (place_in, place), (offset_in, offset), (keys_in, keys), (values_in, values), (queries_in, queries)
    copies = [pltpu.make_async_copy(source, target, sems.at[i]) for i, (source, target) in enumerate(pairs)]
    for copy in copies:
        copy.start()
    copies[0].wait()
    copies[1].wait()
    shape = (ROWS, HEAD_DIM)
    lane = lax.broadcasted_iota(jnp.int32, shape, 1)
    by_place = jnp.broadcast_to(place[...].astype(jnp.float32), shape).T
    by_offset = jnp.broadcast_to(offset[...].astype(jnp.float32), shape).T
    angle = jnp.where(lane < 32, by_place, by_offset) * frequency[...]
    cosine, sine = jnp.cos(angle), jnp.sin(angle)
    first = lane % 32 < 16
    minus = jnp.where(first, -sine, 0.0)
    plus = jnp.where(first, 0.0, sine)
    tables[0], tables[1], tables[2] = cosine, minus, plus
    copies[2].wait()
    copies[3].wait()
    for group in range(2):
        lanes = slice(group * HEAD_DIM, (group + 1) * HEAD_DIM)
        turned = rotate(keys[:, lanes].astype(jnp.float32), cosine, minus, plus).astype(jnp.bfloat16)
        across = values[:, lanes].astype(jnp.float32).T.astype(jnp.bfloat16)
        for x in (group, group + 2):
            for half in range(2):
                payload[2 * x + half, :ROWS, :] = turned
                payload[2 * x + half, ROWS:, :] = across
    copies[4].wait()
    for head in range(HEADS_PER_GROUP):
        cols = slice(head * ROWS, (head + 1) * ROWS)
        turned = rotate(queries[:, cols].astype(jnp.float32), cosine, minus, plus).astype(jnp.bfloat16)
        other[:, cols] = turned.astype(jnp.float32).T.astype(jnp.bfloat16)


def split_queries(x, odd, tip):
    x = x * SCALE
    high = x.astype(jnp.bfloat16)
    guard = jnp.where(tip == HEAD_DIM - 1, NEGATIVE, jnp.where(odd > 0.5, 0.0, NEGATIVE))
    low = jnp.where(tip < HEAD_DIM - 2, x - high.astype(jnp.float32), guard)
    return high, low.astype(jnp.bfloat16)


def turn_queries(queries, tables, group, head):
    start = pl.multiple_of(group * WIDTH + head * HEAD_DIM, HEAD_DIM)
    x = queries[:, pl.ds(start, HEAD_DIM)].astype(jnp.float32)
    return rotate(x, tables[0], tables[1], tables[2]).astype(jnp.bfloat16).astype(jnp.float32).T


def own_queries_kernel(queries, tables, all_segments, own, odds, segments, sem):
    me, uly = lax.axis_index("blk"), lax.axis_index("uly")
    square = (ROWS, ROWS)
    tip = lax.broadcasted_iota(jnp.int32, square, 0)
    base = jnp.clip(me - 2, 0, BLOCKS - 5)
    copy = pltpu.make_async_copy(all_segments.at[pl.ds(base * SHARDS, 5 * SHARDS)], segments, sem)
    copy.start()
    copy.wait()
    odd = jnp.broadcast_to((segments[(me - base) * SHARDS + uly] & 1).astype(jnp.float32), square)
    for head in range(HEADS_PER_GROUP):
        cols = slice(head * ROWS, (head + 1) * ROWS)
        high, low = split_queries(turn_queries(queries, tables, uly // 2 % 2, head), odd, tip)
        own[:HEAD_DIM, cols] = high
        own[HEAD_DIM:, cols] = low

    def chunk_step(c, carry):
        start = pl.multiple_of(c * ROWS, ROWS)
        column = jnp.broadcast_to((segments[c] & 1).astype(jnp.float32), square).T
        odds[pl.ds(start, ROWS), :] = column.astype(jnp.bfloat16)
        return carry

    lax.fori_loop(0, 5 * SHARDS, chunk_step, 0, unroll=4)


def attend_kernel(sets, roles, pairs, start, final, *refs):
    refs = list(refs)
    classes, segments, odds = refs.pop(0), refs.pop(0), refs.pop(0)
    count = len(sets)
    laid = [(refs.pop(0), refs.pop(0)) for _ in range(pairs)]
    if start:
        arrived = refs.pop(0)
        splits = [None, refs.pop(0)]
    else:
        splits = [refs.pop(0) for _ in range(count)]
    blocks = [] if pairs else [refs.pop(0) for _ in roles]
    given = [] if start else [refs.pop(0) for _ in range(count)]
    bias = refs.pop(-1) if start else None
    outs = [refs.pop(0) for _ in range(count)] if final else []
    if final:
        states = refs[-count:]
    else:
        states = [refs.pop(0) for _ in range(count)]
    if start:
        splits[0] = refs.pop(0)
    if not pairs:
        laid = [(refs.pop(0), refs.pop(0))]
    keys = [pair[0].at[i] for pair in laid for i in range(pair[0].shape[0])]
    values = [pair[1].at[i] for pair in laid for i in range(pair[1].shape[0])]

    me, uly = lax.axis_index("blk"), lax.axis_index("uly")
    step = 1 - 2 * (me % 2)
    distance_of = {"own": 0, "near": step, "far": 2 * step, "late": -step, "back": -2 * step}
    klass = classes[me]
    base = jnp.clip(me - 2, 0, BLOCKS - 5)
    square = (ROWS, ROWS)
    lane = lax.broadcasted_iota(jnp.int32, square, 1)
    tip = lax.broadcasted_iota(jnp.int32, square, 0)
    chunks = [partner_of(me, uly) if theirs else uly for theirs in sets]

    def odd_tokens(s, shape):
        segment = segments[(me - base) * SHARDS + chunks[s]]
        return jnp.broadcast_to((segment & 1).astype(jnp.float32), shape)

    def hidden(s, first, number):
        shape = (number, ROWS)
        at = pl.multiple_of((me - base) * BLOCK + first, ROWS)
        context = (odds[pl.ds(at, number), :].astype(jnp.float32) < 0.5) & (klass == 2)
        follows = (odd_tokens(s, shape) > 0.5) | (klass != 2)
        key_at = first + lax.broadcasted_iota(jnp.int32, shape, 0)
        token_at = chunks[s] * ROWS + lax.broadcasted_iota(jnp.int32, shape, 1)
        return jnp.where(context | (follows & (key_at <= token_at)), 0.0, NEGATIVE)

    facts = []
    for role in roles:
        distance = distance_of[role]
        there = me + distance
        seen = (there >= 0) & (there < BLOCKS) & ((klass != 1) | (distance <= 0))
        facts.append((distance, there, seen))

    def lay_out(j):
        distance, there, _ = facts[j]
        before = jnp.where((klass == 2) & (distance < 0), 1.0, 0.0)
        after = jnp.where((klass == 2) & (distance > 0), 1.0, 0.0)
        guard = jnp.where(lane == HEAD_DIM - 2, before, jnp.where(lane == HEAD_DIM - 1, after, 0.0))
        place = jnp.clip(there - base, 0, 4) * SHARDS
        for c in range(SHARDS):
            rows = slice(c * ROWS, (c + 1) * ROWS)
            part = blocks[j][c, :ROWS, :]
            keys[j][rows, :HEAD_DIM] = part
            odd = odds[pl.ds(pl.multiple_of((place + c) * ROWS, ROWS), ROWS), :].astype(jnp.float32)
            part = jnp.where(lane < HEAD_DIM - 2, part.astype(jnp.float32), odd * guard)
            keys[j][rows, HEAD_DIM:] = part.astype(jnp.bfloat16)
            values[j][:, rows] = blocks[j][c, ROWS:, :]

    wide = STACK * ROWS
    items = [
        (s, slice(tile * wide, (tile + 1) * wide)) for s in range(count) for tile in range(HEADS_PER_GROUP // STACK)
    ]

    def scores(j, s, cols):
        return jnp.dot(keys[j][...], splits[s][:, cols], preferred_element_type=jnp.float32)

    def take(which, masked):
        steps = [(j, s, cols) for j in which for s, cols in items]
        tops = [states[s][MAXIMUM : MAXIMUM + 1, :] for s in range(count)]
        ahead = scores(*steps[0])
        for i, (j, s, cols) in enumerate(steps):
            now, ahead = ahead, scores(*steps[i + 1]) if i + 1 < len(steps) else None
            if masked:
                now = now + jnp.concatenate([bias[s]] * STACK, axis=1)
            weights = jnp.exp2(now - tops[s][:, cols])
            part = jnp.dot(values[j][...], weights.astype(jnp.bfloat16), preferred_element_type=jnp.float32)
            states[s][:HEAD_DIM, cols] += part
            states[s][HEAD_DIM : HEAD_DIM + 1, cols] += jnp.sum(weights, axis=0, keepdims=True)

    def take_largest(which, masked):
        def head_step(head, carry):
            cols = pl.ds(pl.multiple_of(head * ROWS, ROWS), ROWS)
            for s in range(count):
                now = scores(which[0], s, cols)
                if masked:
                    now = now + bias[s]
                old = states[s][MAXIMUM : MAXIMUM + 1, cols]
                new = jnp.maximum(old, jnp.max(now, axis=0, keepdims=True))
                decay = jnp.exp2(old - new)
                weights = jnp.exp2(now - new)
                part = jnp.dot(values[which[0]][...], weights.astype(jnp.bfloat16), preferred_element_type=jnp.float32)
                states[s][:HEAD_DIM, cols] = states[s][:HEAD_DIM, cols] * decay + part
                total = states[s][HEAD_DIM : HEAD_DIM + 1, cols] * decay + jnp.sum(weights, axis=0, keepdims=True)
                states[s][HEAD_DIM : HEAD_DIM + 1, cols] = total
                states[s][MAXIMUM : MAXIMUM + 1, cols] = new
            return carry

        lax.fori_loop(0, HEADS_PER_GROUP, head_step, 0)

    def each_block(how):
        for j in range(len(roles)):

            @pl.when(facts[j][2])
            def _(j=j):
                how([j], False)

    def own_block(how):
        @pl.when(klass == 0)
        def _():
            how([0], False)

        @pl.when(klass != 0)
        def _():
            how([0], True)

    if start:
        odd = odd_tokens(0, square)
        for head in range(HEADS_PER_GROUP):
            cols = slice(head * ROWS, (head + 1) * ROWS)
            high, low = split_queries(arrived[:, cols].astype(jnp.float32), odd, tip)
            splits[0][:HEAD_DIM, cols] = high
            splits[0][HEAD_DIM:, cols] = low
        lay_out(0)
        for s in range(count):
            rows = pl.ds(pl.multiple_of(chunks[s] * ROWS, ROWS), ROWS)
            near = jnp.dot(keys[0][rows, :], splits[s][...], preferred_element_type=jnp.float32)
            near = near + jnp.concatenate([hidden(s, chunks[s] * ROWS, ROWS)] * HEADS_PER_GROUP, axis=1)
            states[s][:MAXIMUM, :] = jnp.zeros((MAXIMUM, WIDTH), jnp.float32)
            states[s][MAXIMUM : MAXIMUM + 1, :] = jnp.max(near, axis=0, keepdims=True)

        @pl.when(klass != 0)
        def _():
            for s in range(count):
                bias[s] = hidden(s, 0, BLOCK)

        own_block(take)
    else:
        for j in range(len(blocks)):
            lay_out(j)
        for s in range(count):
            states[s][...] = given[s][...]
        every = facts[0][2]
        for fact in facts[1:]:
            every = every & fact[2]

        @pl.when(every)
        def _():
            take(list(range(len(roles))), False)

        @pl.when(jnp.logical_not(every))
        def _():
            each_block(take)

    largest = states[0][HEAD_DIM : HEAD_DIM + 1, :]
    for s in range(1, count):
        largest = jnp.maximum(largest, states[s][HEAD_DIM : HEAD_DIM + 1, :])

    @pl.when(jnp.logical_not(jnp.max(largest) < 2.0**100))
    def _():
        for s in range(count):
            if start:
                states[s][:MAXIMUM, :] = jnp.zeros((MAXIMUM, WIDTH), jnp.float32)
            else:
                states[s][...] = given[s][...]
        if start:
            own_block(take_largest)
        else:
            each_block(take_largest)

    for s, out in enumerate(outs):
        share = 1.0 / states[s][HEAD_DIM : HEAD_DIM + 1, :]
        for head in range(HEADS_PER_GROUP):
            cols = slice(head * ROWS, (head + 1) * ROWS)
            out[:, cols] = (states[s][:HEAD_DIM, cols] * share[:, cols]).T.astype(jnp.bfloat16)


def combine_kernel(mine, others, out, sems):
    group = lax.axis_index("uly") // 2 % 2
    copies = [
        pltpu.make_async_copy(source, out.at[:, pl.ds(pl.multiple_of(which * WIDTH, WIDTH), WIDTH)], sems.at[i])
        for i, (source, which) in enumerate(((mine, group), (others, 1 - group)))
    ]
    for copy in copies:
        copy.start()
    for copy in copies:
        copy.wait()


def attend(name, classes, segments, odds, sets, splits, blocks=None, laid=(), state=None, final=False):
    roles = tuple(blocks) if blocks else tuple(role for group in laid for role in group[0])
    count, number = len(sets), len(roles)
    start = state is None
    whole = pl.BlockSpec(memory_space=pltpu.VMEM)
    state_shape, split_shape = (MAXIMUM + 8, WIDTH), (2 * HEAD_DIM, WIDTH)
    laid_shapes = [(number, BLOCK, 2 * HEAD_DIM), (number, HEAD_DIM, BLOCK)]
    shapes, scratch = [], []
    if final:
        shapes.append(jax.ShapeDtypeStruct((ROWS, WIDTH), jnp.bfloat16))
        laid_out = [jax.ShapeDtypeStruct(shape, jnp.bfloat16) for shape in laid_shapes] if blocks else []
        scratch += [pltpu.VMEM(state_shape, jnp.float32)] * count
    else:
        shapes += [jax.ShapeDtypeStruct(state_shape, jnp.float32)] * count
        laid_out = [jax.ShapeDtypeStruct(shape, jnp.bfloat16) for shape in laid_shapes] if blocks else []
        if start:
            scratch += [pltpu.VMEM(shape, jnp.bfloat16) for shape in laid_shapes]
            laid_out = []
            shapes.append(jax.ShapeDtypeStruct(split_shape, jnp.bfloat16))
            scratch.append(pltpu.VMEM((count, BLOCK, ROWS), jnp.float32))
    shapes += laid_out
    given = [odds, *(x for group in laid for x in group[1:]), *splits, *(blocks or {}).values(), *(state or ())]
    pairs = count * number * HEADS_PER_GROUP * ROWS * BLOCK
    results = list(
        pl.pallas_call(
            functools.partial(attend_kernel, sets, roles, len(laid), start, final),
            out_shape=shapes,
            in_specs=[pl.BlockSpec(memory_space=pltpu.SMEM)] + [whole] * (1 + len(given)),
            out_specs=[whole] * len(shapes),
            scratch_shapes=scratch,
            compiler_params=VMEM,
            cost_estimate=pl.CostEstimate(flops=8 * pairs * HEAD_DIM, bytes_accessed=2**20, transcendentals=pairs),
            name=name,
        )(classes, segments, *given)
    )
    if laid_out:
        laid = (roles, *results[-2:])
    if start:
        splits = [results[count], splits[1]]
    return splits, results[:count], laid, results[0] if final else None


def shards(queries, key_rows, value_rows, span_place, span_offset, segment_number, block_class):
    vmem, hbm = pl.BlockSpec(memory_space=pltpu.VMEM), pl.BlockSpec(memory_space=pl.ANY)
    payload, tables, q_other = pl.pallas_call(
        keys_kernel,
        out_shape=[
            jax.ShapeDtypeStruct((SHARDS, 2 * ROWS, HEAD_DIM), jnp.bfloat16),
            jax.ShapeDtypeStruct((3, ROWS, HEAD_DIM), jnp.float32),
            jax.ShapeDtypeStruct((HEAD_DIM, WIDTH), jnp.bfloat16),
        ],
        in_specs=[hbm, hbm, vmem, hbm, hbm, hbm],
        out_specs=[vmem, vmem, vmem],
        scratch_shapes=[
            pltpu.VMEM((1, ROWS), jnp.int32),
            pltpu.VMEM((1, ROWS), jnp.int32),
            pltpu.VMEM((ROWS, 2 * HEAD_DIM), jnp.bfloat16),
            pltpu.VMEM((ROWS, 2 * HEAD_DIM), jnp.bfloat16),
            pltpu.VMEM((ROWS, WIDTH), jnp.bfloat16),
            pltpu.SemaphoreType.DMA((5,)),
        ],
        compiler_params=pltpu.CompilerParams(vmem_limit_bytes=KEYS_VMEM),
        name="rotate_keys",
    )(span_place[None, :], span_offset[None, :], lane_frequencies(), key_rows, value_rows, queries)
    own = lax.all_to_all(payload, "uly", split_axis=0, concat_axis=0, tiled=True)

    every = [(b, u) for b in range(BLOCKS) for u in range(SHARDS)]
    partners = [(b * SHARDS + u, b * SHARDS + partner_of(b, u)) for b, u in every]
    q_partner = lax.ppermute(q_other, ("blk", "uly"), partners)
    split_own, odds, segments = pl.pallas_call(
        own_queries_kernel,
        out_shape=[
            jax.ShapeDtypeStruct((2 * HEAD_DIM, WIDTH), jnp.bfloat16),
            jax.ShapeDtypeStruct((5 * BLOCK, ROWS), jnp.bfloat16),
            jax.ShapeDtypeStruct((5 * SHARDS, 1, ROWS), jnp.int32),
        ],
        in_specs=[vmem, vmem, hbm],
        out_specs=[vmem, vmem, vmem],
        scratch_shapes=[pltpu.SemaphoreType.DMA],
        compiler_params=VMEM,
        name="rotate_own_queries",
    )(queries, tables, segment_number.reshape(BLOCKS * SHARDS, 1, ROWS))
    ready = (own, split_own, q_partner, odds, segments)
    own, split_own, q_partner, odds, segments = lax.optimization_barrier(ready)

    within = range(BLOCKS)
    ahead = [(i + 2 - 4 * (i % 2), i) for i in within if i + 2 - 4 * (i % 2) in within]
    behind = [(i - 2 + 4 * (i % 2), i) for i in within if i - 2 + 4 * (i % 2) in within]
    cores = [(i, i ^ 1) for i in within]
    far = lax.ppermute(own, "blk", ahead)
    near = lax.ppermute(own, "blk", cores)

    run = functools.partial(attend, classes=block_class, segments=segments, odds=odds)
    both = (True, False)
    splits, state, _, _ = run("attend_own", sets=both, splits=(q_partner, split_own), blocks={"own": own})
    own, state = lax.optimization_barrier((own, state))
    back = lax.ppermute(own, "blk", behind)
    far, state = lax.optimization_barrier((far, state))
    late = lax.ppermute(far, "blk", cores)
    theirs = functools.partial(run, sets=both[:1], splits=splits[:1])
    _, passed, laid, _ = theirs("attend_near", state=state[:1], blocks={"near": near, "far": far})
    _, _, rest, to_send = theirs("attend_partner", state=passed, blocks={"late": late, "back": back}, final=True)
    others = lax.ppermute(to_send, ("blk", "uly"), partners)
    mine = run("attend_rest", sets=both[1:], splits=splits[1:], state=state[1:], laid=(laid, rest), final=True)[3]
    return pl.pallas_call(
        combine_kernel,
        out_shape=jax.ShapeDtypeStruct((ROWS, 2 * WIDTH), jnp.bfloat16),
        in_specs=[vmem, vmem],
        out_specs=hbm,
        scratch_shapes=[pltpu.SemaphoreType.DMA((2,))],
        compiler_params=VMEM,
        name="combine",
    )(mine, others)


def solution(mesh):
    rows = P(("blk", "uly"), None)
    line = P(("blk", "uly"))
    return jax.shard_map(
        shards,
        mesh=mesh,
        in_specs=(rows, rows, rows, line, line, P(), P()),
        out_specs=rows,
        check_vma=False,
    )
```

```python
import functools

import jax
import jax.numpy as jnp
import numpy as np
from jax import lax
from jax.experimental import pallas as pl
from jax.experimental.pallas import tpu as pltpu
from jax.sharding import PartitionSpec as P

HEAD_DIM = 128
HEADS_PER_GROUP = 8
WIDTH = HEADS_PER_GROUP * HEAD_DIM
ROWS = 128
SHARDS = 8
BLOCK = ROWS * SHARDS
BLOCKS = 64
STACK = 8
NEGATIVE = -1e30
SCALE = HEAD_DIM**-0.5 * 1.4426950408889634
MAXIMUM = HEAD_DIM + 8
VMEM = pltpu.CompilerParams(vmem_limit_bytes=16 * 2**20)
KEYS_VMEM = 60 * 2**20


def lane_frequencies():
    one = 10000.0 ** (-np.arange(16, dtype=np.float64) / 16)
    return np.concatenate([one, one, one, one, np.zeros(64)]).astype(np.float32)[None, :]


def partner_of(block, uly):
    return uly ^ (2 + 4 * (block % 2))


def rotate(x, cosine, minus, plus):
    return (
        x * cosine
        + pltpu.roll(x, HEAD_DIM - 16, axis=1) * minus
        + pltpu.roll(x, 16, axis=1) * plus
    )


def keys_kernel(*refs):
    place_in, offset_in, frequency, keys_in, values_in, queries_in = refs[:6]
    payload, tables, other, place, offset, keys, values, queries, sems = refs[6:]
    group = 1 - lax.axis_index("uly") // 2 % 2
    queries_in = queries_in.at[:, pl.ds(pl.multiple_of(group * WIDTH, WIDTH), WIDTH)]
    pairs = (place_in, place), (offset_in, offset), (keys_in, keys), (values_in, values), (queries_in, queries)
    copies = [pltpu.make_async_copy(source, target, sems.at[i]) for i, (source, target) in enumerate(pairs)]
    for copy in copies:
        copy.start()
    copies[0].wait()
    copies[1].wait()
    shape = (ROWS, HEAD_DIM)
    lane = lax.broadcasted_iota(jnp.int32, shape, 1)
    by_place = jnp.broadcast_to(place[...].astype(jnp.float32), shape).T
    by_offset = jnp.broadcast_to(offset[...].astype(jnp.float32), shape).T
    angle = jnp.where(lane < 32, by_place, by_offset) * frequency[...]
    cosine, sine = jnp.cos(angle), jnp.sin(angle)
    first = lane % 32 < 16
    minus = jnp.where(first, -sine, 0.0)
    plus = jnp.where(first, 0.0, sine)
    tables[0], tables[1], tables[2] = cosine, minus, plus
    copies[2].wait()
    copies[3].wait()
    for group in range(2):
        lanes = slice(group * HEAD_DIM, (group + 1) * HEAD_DIM)
        turned = rotate(keys[:, lanes].astype(jnp.float32), cosine, minus, plus).astype(jnp.bfloat16)
        across = values[:, lanes].astype(jnp.float32).T.astype(jnp.bfloat16)
        for x in (group, group + 2):
            for half in range(2):
                payload[2 * x + half, :ROWS, :] = turned
                payload[2 * x + half, ROWS:, :] = across
    copies[4].wait()
    for head in range(HEADS_PER_GROUP):
        cols = slice(head * ROWS, (head + 1) * ROWS)
        turned = rotate(queries[:, cols].astype(jnp.float32), cosine, minus, plus).astype(jnp.bfloat16)
        other[:, cols] = turned.astype(jnp.float32).T.astype(jnp.bfloat16)


def split_queries(x, odd, tip):
    x = x * SCALE
    high = x.astype(jnp.bfloat16)
    guard = jnp.where(tip == HEAD_DIM - 1, NEGATIVE, jnp.where(odd > 0.5, 0.0, NEGATIVE))
    low = jnp.where(tip < HEAD_DIM - 2, x - high.astype(jnp.float32), guard)
    return high, low.astype(jnp.bfloat16)


def turn_queries(queries, tables, group, head):
    start = pl.multiple_of(group * WIDTH + head * HEAD_DIM, HEAD_DIM)
    x = queries[:, pl.ds(start, HEAD_DIM)].astype(jnp.float32)
    return rotate(x, tables[0], tables[1], tables[2]).astype(jnp.bfloat16).astype(jnp.float32).T


def own_queries_kernel(queries, tables, all_segments, own, odds, segments, sem):
    me, uly = lax.axis_index("blk"), lax.axis_index("uly")
    square = (ROWS, ROWS)
    tip = lax.broadcasted_iota(jnp.int32, square, 0)
    base = jnp.clip(me - 2, 0, BLOCKS - 5)
    copy = pltpu.make_async_copy(all_segments.at[pl.ds(base * SHARDS, 5 * SHARDS)], segments, sem)
    copy.start()
    copy.wait()
    odd = jnp.broadcast_to((segments[(me - base) * SHARDS + uly] & 1).astype(jnp.float32), square)
    for head in range(HEADS_PER_GROUP):
        cols = slice(head * ROWS, (head + 1) * ROWS)
        high, low = split_queries(turn_queries(queries, tables, uly // 2 % 2, head), odd, tip)
        own[:HEAD_DIM, cols] = high
        own[HEAD_DIM:, cols] = low

    def chunk_step(c, carry):
        start = pl.multiple_of(c * ROWS, ROWS)
        column = jnp.broadcast_to((segments[c] & 1).astype(jnp.float32), square).T
        odds[pl.ds(start, ROWS), :] = column.astype(jnp.bfloat16)
        return carry

    lax.fori_loop(0, 5 * SHARDS, chunk_step, 0, unroll=4)


def attend_kernel(sets, roles, pairs, start, final, *refs):
    refs = list(refs)
    classes, segments, odds = refs.pop(0), refs.pop(0), refs.pop(0)
    count = len(sets)
    laid = [(refs.pop(0), refs.pop(0)) for _ in range(pairs)]
    if start:
        arrived = refs.pop(0)
        splits = [None, refs.pop(0)]
    else:
        splits = [refs.pop(0) for _ in range(count)]
    blocks = [] if pairs else [refs.pop(0) for _ in roles]
    given = [] if start else [refs.pop(0) for _ in range(count)]
    bias = refs.pop(-1) if start else None
    outs = [refs.pop(0) for _ in range(count)] if final else []
    if final:
        states = refs[-count:]
    else:
        states = [refs.pop(0) for _ in range(count)]
    if start:
        splits[0] = refs.pop(0)
    if not pairs:
        laid = [(refs.pop(0), refs.pop(0))]
    keys = [pair[0].at[i] for pair in laid for i in range(pair[0].shape[0])]
    values = [pair[1].at[i] for pair in laid for i in range(pair[1].shape[0])]

    me, uly = lax.axis_index("blk"), lax.axis_index("uly")
    step = 1 - 2 * (me % 2)
    distance_of = {"own": 0, "near": step, "far": 2 * step, "late": -step, "back": -2 * step}
    klass = classes[me]
    base = jnp.clip(me - 2, 0, BLOCKS - 5)
    square = (ROWS, ROWS)
    lane = lax.broadcasted_iota(jnp.int32, square, 1)
    tip = lax.broadcasted_iota(jnp.int32, square, 0)
    chunks = [partner_of(me, uly) if theirs else uly for theirs in sets]

    def odd_tokens(s, shape):
        segment = segments[(me - base) * SHARDS + chunks[s]]
        return jnp.broadcast_to((segment & 1).astype(jnp.float32), shape)

    def hidden(s, first, number):
        shape = (number, ROWS)
        at = pl.multiple_of((me - base) * BLOCK + first, ROWS)
        context = (odds[pl.ds(at, number), :].astype(jnp.float32) < 0.5) & (klass == 2)
        follows = (odd_tokens(s, shape) > 0.5) | (klass != 2)
        key_at = first + lax.broadcasted_iota(jnp.int32, shape, 0)
        token_at = chunks[s] * ROWS + lax.broadcasted_iota(jnp.int32, shape, 1)
        return jnp.where(context | (follows & (key_at <= token_at)), 0.0, NEGATIVE)

    facts = []
    for role in roles:
        distance = distance_of[role]
        there = me + distance
        seen = (there >= 0) & (there < BLOCKS) & ((klass != 1) | (distance <= 0))
        facts.append((distance, there, seen))

    def lay_out(j):
        distance, there, _ = facts[j]
        before = jnp.where((klass == 2) & (distance < 0), 1.0, 0.0)
        after = jnp.where((klass == 2) & (distance > 0), 1.0, 0.0)
        guard = jnp.where(lane == HEAD_DIM - 2, before, jnp.where(lane == HEAD_DIM - 1, after, 0.0))
        place = jnp.clip(there - base, 0, 4) * SHARDS
        for c in range(SHARDS):
            rows = slice(c * ROWS, (c + 1) * ROWS)
            part = blocks[j][c, :ROWS, :]
            keys[j][rows, :HEAD_DIM] = part
            odd = odds[pl.ds(pl.multiple_of((place + c) * ROWS, ROWS), ROWS), :].astype(jnp.float32)
            part = jnp.where(lane < HEAD_DIM - 2, part.astype(jnp.float32), odd * guard)
            keys[j][rows, HEAD_DIM:] = part.astype(jnp.bfloat16)
            values[j][:, rows] = blocks[j][c, ROWS:, :]

    wide = STACK * ROWS
    items = [
        (s, slice(tile * wide, (tile + 1) * wide)) for s in range(count) for tile in range(HEADS_PER_GROUP // STACK)
    ]

    def scores(j, s, cols):
        return jnp.dot(keys[j][...], splits[s][:, cols], preferred_element_type=jnp.float32)

    def take(which, masked):
        steps = [(j, s, cols) for j in which for s, cols in items]
        tops = [states[s][MAXIMUM : MAXIMUM + 1, :] for s in range(count)]
        ahead = scores(*steps[0])
        for i, (j, s, cols) in enumerate(steps):
            now, ahead = ahead, scores(*steps[i + 1]) if i + 1 < len(steps) else None
            if masked:
                now = now + jnp.concatenate([bias[s]] * STACK, axis=1)
            weights = jnp.exp2(now - tops[s][:, cols])
            part = jnp.dot(values[j][...], weights.astype(jnp.bfloat16), preferred_element_type=jnp.float32)
            states[s][:HEAD_DIM, cols] += part
            states[s][HEAD_DIM : HEAD_DIM + 1, cols] += jnp.sum(weights, axis=0, keepdims=True)

    def take_largest(which, masked):
        def head_step(head, carry):
            cols = pl.ds(pl.multiple_of(head * ROWS, ROWS), ROWS)
            for s in range(count):
                now = scores(which[0], s, cols)
                if masked:
                    now = now + bias[s]
                old = states[s][MAXIMUM : MAXIMUM + 1, cols]
                new = jnp.maximum(old, jnp.max(now, axis=0, keepdims=True))
                decay = jnp.exp2(old - new)
                weights = jnp.exp2(now - new)
                part = jnp.dot(values[which[0]][...], weights.astype(jnp.bfloat16), preferred_element_type=jnp.float32)
                states[s][:HEAD_DIM, cols] = states[s][:HEAD_DIM, cols] * decay + part
                total = states[s][HEAD_DIM : HEAD_DIM + 1, cols] * decay + jnp.sum(weights, axis=0, keepdims=True)
                states[s][HEAD_DIM : HEAD_DIM + 1, cols] = total
                states[s][MAXIMUM : MAXIMUM + 1, cols] = new
            return carry

        lax.fori_loop(0, HEADS_PER_GROUP, head_step, 0)

    def each_block(how):
        for j in range(len(roles)):

            @pl.when(facts[j][2])
            def _(j=j):
                how([j], False)

    def own_block(how):
        @pl.when(klass == 0)
        def _():
            how([0], False)

        @pl.when(klass != 0)
        def _():
            how([0], True)

    if start:
        odd = odd_tokens(0, square)
        for head in range(HEADS_PER_GROUP):
            cols = slice(head * ROWS, (head + 1) * ROWS)
            high, low = split_queries(arrived[:, cols].astype(jnp.float32), odd, tip)
            splits[0][:HEAD_DIM, cols] = high
            splits[0][HEAD_DIM:, cols] = low
        lay_out(0)
        for s in range(count):
            rows = pl.ds(pl.multiple_of(chunks[s] * ROWS, ROWS), ROWS)
            near = jnp.dot(keys[0][rows, :], splits[s][...], preferred_element_type=jnp.float32)
            near = near + jnp.concatenate([hidden(s, chunks[s] * ROWS, ROWS)] * HEADS_PER_GROUP, axis=1)
            states[s][:MAXIMUM, :] = jnp.zeros((MAXIMUM, WIDTH), jnp.float32)
            states[s][MAXIMUM : MAXIMUM + 1, :] = jnp.max(near, axis=0, keepdims=True)

        @pl.when(klass != 0)
        def _():
            for s in range(count):
                bias[s] = hidden(s, 0, BLOCK)

        own_block(take)
    else:
        for j in range(len(blocks)):
            lay_out(j)
        for s in range(count):
            states[s][...] = given[s][...]
        every = facts[0][2]
        for fact in facts[1:]:
            every = every & fact[2]

        @pl.when(every)
        def _():
            take(list(range(len(roles))), False)

        @pl.when(jnp.logical_not(every))
        def _():
            each_block(take)

    largest = states[0][HEAD_DIM : HEAD_DIM + 1, :]
    for s in range(1, count):
        largest = jnp.maximum(largest, states[s][HEAD_DIM : HEAD_DIM + 1, :])

    @pl.when(jnp.logical_not(jnp.max(largest) < 2.0**100))
    def _():
        for s in range(count):
            if start:
                states[s][:MAXIMUM, :] = jnp.zeros((MAXIMUM, WIDTH), jnp.float32)
            else:
                states[s][...] = given[s][...]
        if start:
            own_block(take_largest)
        else:
            each_block(take_largest)

    for s, out in enumerate(outs):
        share = 1.0 / states[s][HEAD_DIM : HEAD_DIM + 1, :]
        for head in range(HEADS_PER_GROUP):
            cols = slice(head * ROWS, (head + 1) * ROWS)
            out[:, cols] = (states[s][:HEAD_DIM, cols] * share[:, cols]).T.astype(jnp.bfloat16)


def combine_kernel(mine, others, out, sems):
    group = lax.axis_index("uly") // 2 % 2
    copies = [
        pltpu.make_async_copy(source, out.at[:, pl.ds(pl.multiple_of(which * WIDTH, WIDTH), WIDTH)], sems.at[i])
        for i, (source, which) in enumerate(((mine, group), (others, 1 - group)))
    ]
    for copy in copies:
        copy.start()
    for copy in copies:
        copy.wait()


def attend(name, classes, segments, odds, sets, splits, blocks=None, laid=(), state=None, final=False):
    roles = tuple(blocks) if blocks else tuple(role for group in laid for role in group[0])
    count, number = len(sets), len(roles)
    start = state is None
    whole = pl.BlockSpec(memory_space=pltpu.VMEM)
    state_shape, split_shape = (MAXIMUM + 8, WIDTH), (2 * HEAD_DIM, WIDTH)
    laid_shapes = [(number, BLOCK, 2 * HEAD_DIM), (number, HEAD_DIM, BLOCK)]
    shapes, scratch = [], []
    if final:
        shapes.append(jax.ShapeDtypeStruct((ROWS, WIDTH), jnp.bfloat16))
        laid_out = [jax.ShapeDtypeStruct(shape, jnp.bfloat16) for shape in laid_shapes] if blocks else []
        scratch += [pltpu.VMEM(state_shape, jnp.float32)] * count
    else:
        shapes += [jax.ShapeDtypeStruct(state_shape, jnp.float32)] * count
        laid_out = [jax.ShapeDtypeStruct(shape, jnp.bfloat16) for shape in laid_shapes] if blocks else []
        if start:
            scratch += [pltpu.VMEM(shape, jnp.bfloat16) for shape in laid_shapes]
            laid_out = []
            shapes.append(jax.ShapeDtypeStruct(split_shape, jnp.bfloat16))
            scratch.append(pltpu.VMEM((count, BLOCK, ROWS), jnp.float32))
    shapes += laid_out
    given = [odds, *(x for group in laid for x in group[1:]), *splits, *(blocks or {}).values(), *(state or ())]
    pairs = count * number * HEADS_PER_GROUP * ROWS * BLOCK
    results = list(
        pl.pallas_call(
            functools.partial(attend_kernel, sets, roles, len(laid), start, final),
            out_shape=shapes,
            in_specs=[pl.BlockSpec(memory_space=pltpu.SMEM)] + [whole] * (1 + len(given)),
            out_specs=[whole] * len(shapes),
            scratch_shapes=scratch,
            compiler_params=VMEM,
            cost_estimate=pl.CostEstimate(flops=8 * pairs * HEAD_DIM, bytes_accessed=2**20, transcendentals=pairs),
            name=name,
        )(classes, segments, *given)
    )
    if laid_out:
        laid = (roles, *results[-2:])
    if start:
        splits = [results[count], splits[1]]
    return splits, results[:count], laid, results[0] if final else None


def shards(queries, key_rows, value_rows, span_place, span_offset, segment_number, block_class):
    vmem, hbm = pl.BlockSpec(memory_space=pltpu.VMEM), pl.BlockSpec(memory_space=pl.ANY)
    payload, tables, q_other = pl.pallas_call(
        keys_kernel,
        out_shape=[
            jax.ShapeDtypeStruct((SHARDS, 2 * ROWS, HEAD_DIM), jnp.bfloat16),
            jax.ShapeDtypeStruct((3, ROWS, HEAD_DIM), jnp.float32),
            jax.ShapeDtypeStruct((HEAD_DIM, WIDTH), jnp.bfloat16),
        ],
        in_specs=[hbm, hbm, vmem, hbm, hbm, hbm],
        out_specs=[vmem, vmem, vmem],
        scratch_shapes=[
            pltpu.VMEM((1, ROWS), jnp.int32),
            pltpu.VMEM((1, ROWS), jnp.int32),
            pltpu.VMEM((ROWS, 2 * HEAD_DIM), jnp.bfloat16),
            pltpu.VMEM((ROWS, 2 * HEAD_DIM), jnp.bfloat16),
            pltpu.VMEM((ROWS, WIDTH), jnp.bfloat16),
            pltpu.SemaphoreType.DMA((5,)),
        ],
        compiler_params=pltpu.CompilerParams(vmem_limit_bytes=KEYS_VMEM),
        name="rotate_keys",
    )(span_place[None, :], span_offset[None, :], lane_frequencies(), key_rows, value_rows, queries)
    own = lax.all_to_all(payload, "uly", split_axis=0, concat_axis=0, tiled=True)

    every = [(b, u) for b in range(BLOCKS) for u in range(SHARDS)]
    partners = [(b * SHARDS + u, b * SHARDS + partner_of(b, u)) for b, u in every]
    q_partner = lax.ppermute(q_other, ("blk", "uly"), partners)
    split_own, odds, segments = pl.pallas_call(
        own_queries_kernel,
        out_shape=[
            jax.ShapeDtypeStruct((2 * HEAD_DIM, WIDTH), jnp.bfloat16),
            jax.ShapeDtypeStruct((5 * BLOCK, ROWS), jnp.bfloat16),
            jax.ShapeDtypeStruct((5 * SHARDS, 1, ROWS), jnp.int32),
        ],
        in_specs=[vmem, vmem, hbm],
        out_specs=[vmem, vmem, vmem],
        scratch_shapes=[pltpu.SemaphoreType.DMA],
        compiler_params=VMEM,
        name="rotate_own_queries",
    )(queries, tables, segment_number.reshape(BLOCKS * SHARDS, 1, ROWS))
    ready = (own, split_own, q_partner, odds, segments)
    own, split_own, q_partner, odds, segments = lax.optimization_barrier(ready)

    within = range(BLOCKS)
    ahead = [(i + 2 - 4 * (i % 2), i) for i in within if i + 2 - 4 * (i % 2) in within]
    behind = [(i - 2 + 4 * (i % 2), i) for i in within if i - 2 + 4 * (i % 2) in within]
    cores = [(i, i ^ 1) for i in within]
    far = lax.ppermute(own, "blk", ahead)

    run = functools.partial(attend, classes=block_class, segments=segments, odds=odds)
    both = (True, False)
    splits, state, _, _ = run("attend_own", sets=both, splits=(q_partner, split_own), blocks={"own": own})
    own, state = lax.optimization_barrier((own, state))
    back = lax.ppermute(own, "blk", behind)
    near = lax.ppermute(own, "blk", cores)
    far, state = lax.optimization_barrier((far, state))
    late = lax.ppermute(far, "blk", cores)
    theirs = functools.partial(run, sets=both[:1], splits=splits[:1])
    _, passed, laid, _ = theirs("attend_near", state=state[:1], blocks={"near": near, "far": far})
    _, _, rest, to_send = theirs("attend_partner", state=passed, blocks={"late": late, "back": back}, final=True)
    others = lax.ppermute(to_send, ("blk", "uly"), partners)
    mine = run("attend_rest", sets=both[1:], splits=splits[1:], state=state[1:], laid=(laid, rest), final=True)[3]
    return pl.pallas_call(
        combine_kernel,
        out_shape=jax.ShapeDtypeStruct((ROWS, 2 * WIDTH), jnp.bfloat16),
        in_specs=[vmem, vmem],
        out_specs=hbm,
        scratch_shapes=[pltpu.SemaphoreType.DMA((2,))],
        compiler_params=VMEM,
        name="combine",
    )(mine, others)


def solution(mesh):
    rows = P(("blk", "uly"), None)
    line = P(("blk", "uly"))
    return jax.shard_map(
        shards,
        mesh=mesh,
        in_specs=(rows, rows, rows, line, line, P(), P()),
        out_specs=rows,
        check_vma=False,
    )
```

```python
import functools

import jax
import jax.numpy as jnp
import numpy as np
from jax import lax
from jax.experimental import pallas as pl
from jax.experimental.pallas import tpu as pltpu
from jax.sharding import PartitionSpec as P

HEAD_DIM = 128
HEADS_PER_GROUP = 8
WIDTH = HEADS_PER_GROUP * HEAD_DIM
ROWS = 128
SHARDS = 8
BLOCK = ROWS * SHARDS
BLOCKS = 64
STACK = 8
NEGATIVE = -1e30
SCALE = HEAD_DIM**-0.5 * 1.4426950408889634
MAXIMUM = HEAD_DIM + 8
VMEM = pltpu.CompilerParams(vmem_limit_bytes=16 * 2**20)
KEYS_VMEM = 60 * 2**20


def lane_frequencies():
    one = 10000.0 ** (-np.arange(16, dtype=np.float64) / 16)
    return np.concatenate([one, one, one, one, np.zeros(64)]).astype(np.float32)[None, :]


def partner_of(block, uly):
    return uly ^ (2 + 4 * (block % 2))


def rotate(x, cosine, minus, plus):
    return (
        x * cosine
        + pltpu.roll(x, HEAD_DIM - 16, axis=1) * minus
        + pltpu.roll(x, 16, axis=1) * plus
    )


def keys_kernel(*refs):
    place_in, offset_in, frequency, keys_in, values_in, queries_in = refs[:6]
    payload, tables, other, place, offset, keys, values, queries, sems = refs[6:]
    group = 1 - lax.axis_index("uly") // 2 % 2
    queries_in = queries_in.at[:, pl.ds(pl.multiple_of(group * WIDTH, WIDTH), WIDTH)]
    pairs = (place_in, place), (offset_in, offset), (keys_in, keys), (values_in, values), (queries_in, queries)
    copies = [pltpu.make_async_copy(source, target, sems.at[i]) for i, (source, target) in enumerate(pairs)]
    for copy in copies:
        copy.start()
    copies[0].wait()
    copies[1].wait()
    shape = (ROWS, HEAD_DIM)
    lane = lax.broadcasted_iota(jnp.int32, shape, 1)
    by_place = jnp.broadcast_to(place[...].astype(jnp.float32), shape).T
    by_offset = jnp.broadcast_to(offset[...].astype(jnp.float32), shape).T
    angle = jnp.where(lane < 32, by_place, by_offset) * frequency[...]
    cosine, sine = jnp.cos(angle), jnp.sin(angle)
    first = lane % 32 < 16
    minus = jnp.where(first, -sine, 0.0)
    plus = jnp.where(first, 0.0, sine)
    tables[0], tables[1], tables[2] = cosine, minus, plus
    copies[2].wait()
    copies[3].wait()
    for group in range(2):
        lanes = slice(group * HEAD_DIM, (group + 1) * HEAD_DIM)
        turned = rotate(keys[:, lanes].astype(jnp.float32), cosine, minus, plus).astype(jnp.bfloat16)
        across = values[:, lanes].astype(jnp.float32).T.astype(jnp.bfloat16)
        for x in (group, group + 2):
            for half in range(2):
                payload[2 * x + half, :ROWS, :] = turned
                payload[2 * x + half, ROWS:, :] = across
    copies[4].wait()
    for head in range(HEADS_PER_GROUP):
        cols = slice(head * ROWS, (head + 1) * ROWS)
        turned = rotate(queries[:, cols].astype(jnp.float32), cosine, minus, plus).astype(jnp.bfloat16)
        other[:, cols] = turned.astype(jnp.float32).T.astype(jnp.bfloat16)


def split_queries(x, odd, tip):
    x = x * SCALE
    high = x.astype(jnp.bfloat16)
    guard = jnp.where(tip == HEAD_DIM - 1, NEGATIVE, jnp.where(odd > 0.5, 0.0, NEGATIVE))
    low = jnp.where(tip < HEAD_DIM - 2, x - high.astype(jnp.float32), guard)
    return high, low.astype(jnp.bfloat16)


def turn_queries(queries, tables, group, head):
    start = pl.multiple_of(group * WIDTH + head * HEAD_DIM, HEAD_DIM)
    x = queries[:, pl.ds(start, HEAD_DIM)].astype(jnp.float32)
    return rotate(x, tables[0], tables[1], tables[2]).astype(jnp.bfloat16).astype(jnp.float32).T


def own_queries_kernel(queries, tables, all_segments, own, odds, segments, sem):
    me, uly = lax.axis_index("blk"), lax.axis_index("uly")
    square = (ROWS, ROWS)
    tip = lax.broadcasted_iota(jnp.int32, square, 0)
    base = jnp.clip(me - 2, 0, BLOCKS - 5)
    copy = pltpu.make_async_copy(all_segments.at[pl.ds(base * SHARDS, 5 * SHARDS)], segments, sem)
    copy.start()
    copy.wait()
    odd = jnp.broadcast_to((segments[(me - base) * SHARDS + uly] & 1).astype(jnp.float32), square)
    for head in range(HEADS_PER_GROUP):
        cols = slice(head * ROWS, (head + 1) * ROWS)
        high, low = split_queries(turn_queries(queries, tables, uly // 2 % 2, head), odd, tip)
        own[:HEAD_DIM, cols] = high
        own[HEAD_DIM:, cols] = low

    def chunk_step(c, carry):
        start = pl.multiple_of(c * ROWS, ROWS)
        column = jnp.broadcast_to((segments[c] & 1).astype(jnp.float32), square).T
        odds[pl.ds(start, ROWS), :] = column.astype(jnp.bfloat16)
        return carry

    lax.fori_loop(0, 5 * SHARDS, chunk_step, 0, unroll=4)


def attend_kernel(sets, roles, pairs, start, final, *refs):
    refs = list(refs)
    classes, segments, odds = refs.pop(0), refs.pop(0), refs.pop(0)
    count = len(sets)
    laid = [(refs.pop(0), refs.pop(0)) for _ in range(pairs)]
    if start:
        arrived = refs.pop(0)
        splits = [None, refs.pop(0)]
    else:
        splits = [refs.pop(0) for _ in range(count)]
    blocks = [] if pairs else [refs.pop(0) for _ in roles]
    given = [] if start else [refs.pop(0) for _ in range(count)]
    bias = refs.pop(-1) if start else None
    outs = [refs.pop(0) for _ in range(count)] if final else []
    if final:
        states = refs[-count:]
    else:
        states = [refs.pop(0) for _ in range(count)]
    if start:
        splits[0] = refs.pop(0)
    if not pairs:
        laid = [(refs.pop(0), refs.pop(0))]
    keys = [pair[0].at[i] for pair in laid for i in range(pair[0].shape[0])]
    values = [pair[1].at[i] for pair in laid for i in range(pair[1].shape[0])]

    me, uly = lax.axis_index("blk"), lax.axis_index("uly")
    step = 1 - 2 * (me % 2)
    distance_of = {"own": 0, "near": step, "far": 2 * step, "late": -step, "back": -2 * step}
    klass = classes[me]
    base = jnp.clip(me - 2, 0, BLOCKS - 5)
    square = (ROWS, ROWS)
    lane = lax.broadcasted_iota(jnp.int32, square, 1)
    tip = lax.broadcasted_iota(jnp.int32, square, 0)
    chunks = [partner_of(me, uly) if theirs else uly for theirs in sets]

    def odd_tokens(s, shape):
        segment = segments[(me - base) * SHARDS + chunks[s]]
        return jnp.broadcast_to((segment & 1).astype(jnp.float32), shape)

    def hidden(s, first, number):
        shape = (number, ROWS)
        at = pl.multiple_of((me - base) * BLOCK + first, ROWS)
        context = (odds[pl.ds(at, number), :].astype(jnp.float32) < 0.5) & (klass == 2)
        follows = (odd_tokens(s, shape) > 0.5) | (klass != 2)
        key_at = first + lax.broadcasted_iota(jnp.int32, shape, 0)
        token_at = chunks[s] * ROWS + lax.broadcasted_iota(jnp.int32, shape, 1)
        return jnp.where(context | (follows & (key_at <= token_at)), 0.0, NEGATIVE)

    facts = []
    for role in roles:
        distance = distance_of[role]
        there = me + distance
        seen = (there >= 0) & (there < BLOCKS) & ((klass != 1) | (distance <= 0))
        facts.append((distance, there, seen))

    def lay_out(j):
        distance, there, _ = facts[j]
        before = jnp.where((klass == 2) & (distance < 0), 1.0, 0.0)
        after = jnp.where((klass == 2) & (distance > 0), 1.0, 0.0)
        guard = jnp.where(lane == HEAD_DIM - 2, before, jnp.where(lane == HEAD_DIM - 1, after, 0.0))
        place = jnp.clip(there - base, 0, 4) * SHARDS
        for c in range(SHARDS):
            rows = slice(c * ROWS, (c + 1) * ROWS)
            part = blocks[j][c, :ROWS, :]
            keys[j][rows, :HEAD_DIM] = part
            odd = odds[pl.ds(pl.multiple_of((place + c) * ROWS, ROWS), ROWS), :].astype(jnp.float32)
            part = jnp.where(lane < HEAD_DIM - 2, part.astype(jnp.float32), odd * guard)
            keys[j][rows, HEAD_DIM:] = part.astype(jnp.bfloat16)
            values[j][:, rows] = blocks[j][c, ROWS:, :]

    wide = STACK * ROWS
    items = [
        (s, slice(tile * wide, (tile + 1) * wide)) for s in range(count) for tile in range(HEADS_PER_GROUP // STACK)
    ]

    def scores(j, s, cols):
        return jnp.dot(keys[j][...], splits[s][:, cols], preferred_element_type=jnp.float32)

    def take(which, masked):
        steps = [(j, s, cols) for j in which for s, cols in items]
        tops = [states[s][MAXIMUM : MAXIMUM + 1, :] for s in range(count)]
        ahead = scores(*steps[0])
        for i, (j, s, cols) in enumerate(steps):
            now, ahead = ahead, scores(*steps[i + 1]) if i + 1 < len(steps) else None
            if masked:
                now = now + jnp.concatenate([bias[s]] * STACK, axis=1)
            weights = jnp.exp2(now - tops[s][:, cols])
            part = jnp.dot(values[j][...], weights.astype(jnp.bfloat16), preferred_element_type=jnp.float32)
            states[s][:HEAD_DIM, cols] += part
            states[s][HEAD_DIM : HEAD_DIM + 1, cols] += jnp.sum(weights, axis=0, keepdims=True)

    def take_largest(which, masked):
        def head_step(head, carry):
            cols = pl.ds(pl.multiple_of(head * ROWS, ROWS), ROWS)
            for s in range(count):
                now = scores(which[0], s, cols)
                if masked:
                    now = now + bias[s]
                old = states[s][MAXIMUM : MAXIMUM + 1, cols]
                new = jnp.maximum(old, jnp.max(now, axis=0, keepdims=True))
                decay = jnp.exp2(old - new)
                weights = jnp.exp2(now - new)
                part = jnp.dot(values[which[0]][...], weights.astype(jnp.bfloat16), preferred_element_type=jnp.float32)
                states[s][:HEAD_DIM, cols] = states[s][:HEAD_DIM, cols] * decay + part
                total = states[s][HEAD_DIM : HEAD_DIM + 1, cols] * decay + jnp.sum(weights, axis=0, keepdims=True)
                states[s][HEAD_DIM : HEAD_DIM + 1, cols] = total
                states[s][MAXIMUM : MAXIMUM + 1, cols] = new
            return carry

        lax.fori_loop(0, HEADS_PER_GROUP, head_step, 0)

    def each_block(how):
        for j in range(len(roles)):

            @pl.when(facts[j][2])
            def _(j=j):
                how([j], False)

    def own_block(how):
        @pl.when(klass == 0)
        def _():
            how([0], False)

        @pl.when(klass != 0)
        def _():
            how([0], True)

    if start:
        odd = odd_tokens(0, square)
        for head in range(HEADS_PER_GROUP):
            cols = slice(head * ROWS, (head + 1) * ROWS)
            high, low = split_queries(arrived[:, cols].astype(jnp.float32), odd, tip)
            splits[0][:HEAD_DIM, cols] = high
            splits[0][HEAD_DIM:, cols] = low
        lay_out(0)
        for s in range(count):
            rows = pl.ds(pl.multiple_of(chunks[s] * ROWS, ROWS), ROWS)
            near = jnp.dot(keys[0][rows, :], splits[s][...], preferred_element_type=jnp.float32)
            near = near + jnp.concatenate([hidden(s, chunks[s] * ROWS, ROWS)] * HEADS_PER_GROUP, axis=1)
            states[s][:MAXIMUM, :] = jnp.zeros((MAXIMUM, WIDTH), jnp.float32)
            states[s][MAXIMUM : MAXIMUM + 1, :] = jnp.max(near, axis=0, keepdims=True)

        @pl.when(klass != 0)
        def _():
            for s in range(count):
                bias[s] = hidden(s, 0, BLOCK)

        own_block(take)
    else:
        for j in range(len(blocks)):
            lay_out(j)
        for s in range(count):
            states[s][...] = given[s][...]
        every = facts[0][2]
        for fact in facts[1:]:
            every = every & fact[2]

        @pl.when(every)
        def _():
            take(list(range(len(roles))), False)

        @pl.when(jnp.logical_not(every))
        def _():
            each_block(take)

    largest = states[0][HEAD_DIM : HEAD_DIM + 1, :]
    for s in range(1, count):
        largest = jnp.maximum(largest, states[s][HEAD_DIM : HEAD_DIM + 1, :])

    @pl.when(jnp.logical_not(jnp.max(largest) < 2.0**100))
    def _():
        for s in range(count):
            if start:
                states[s][:MAXIMUM, :] = jnp.zeros((MAXIMUM, WIDTH), jnp.float32)
            else:
                states[s][...] = given[s][...]
        if start:
            own_block(take_largest)
        else:
            each_block(take_largest)

    for s, out in enumerate(outs):
        share = 1.0 / states[s][HEAD_DIM : HEAD_DIM + 1, :]
        for head in range(HEADS_PER_GROUP):
            cols = slice(head * ROWS, (head + 1) * ROWS)
            out[:, cols] = (states[s][:HEAD_DIM, cols] * share[:, cols]).T.astype(jnp.bfloat16)


def combine_kernel(mine, others, out, sems):
    group = lax.axis_index("uly") // 2 % 2
    copies = [
        pltpu.make_async_copy(source, out.at[:, pl.ds(pl.multiple_of(which * WIDTH, WIDTH), WIDTH)], sems.at[i])
        for i, (source, which) in enumerate(((mine, group), (others, 1 - group)))
    ]
    for copy in copies:
        copy.start()
    for copy in copies:
        copy.wait()


def attend(name, classes, segments, odds, sets, splits, blocks=None, laid=(), state=None, final=False):
    roles = tuple(blocks) if blocks else tuple(role for group in laid for role in group[0])
    count, number = len(sets), len(roles)
    start = state is None
    whole = pl.BlockSpec(memory_space=pltpu.VMEM)
    state_shape, split_shape = (MAXIMUM + 8, WIDTH), (2 * HEAD_DIM, WIDTH)
    laid_shapes = [(number, BLOCK, 2 * HEAD_DIM), (number, HEAD_DIM, BLOCK)]
    shapes, scratch = [], []
    if final:
        shapes.append(jax.ShapeDtypeStruct((ROWS, WIDTH), jnp.bfloat16))
        laid_out = [jax.ShapeDtypeStruct(shape, jnp.bfloat16) for shape in laid_shapes] if blocks else []
        scratch += [pltpu.VMEM(state_shape, jnp.float32)] * count
    else:
        shapes += [jax.ShapeDtypeStruct(state_shape, jnp.float32)] * count
        laid_out = [jax.ShapeDtypeStruct(shape, jnp.bfloat16) for shape in laid_shapes] if blocks else []
        if start:
            scratch += [pltpu.VMEM(shape, jnp.bfloat16) for shape in laid_shapes]
            laid_out = []
            shapes.append(jax.ShapeDtypeStruct(split_shape, jnp.bfloat16))
            scratch.append(pltpu.VMEM((count, BLOCK, ROWS), jnp.float32))
    shapes += laid_out
    given = [odds, *(x for group in laid for x in group[1:]), *splits, *(blocks or {}).values(), *(state or ())]
    pairs = count * number * HEADS_PER_GROUP * ROWS * BLOCK
    results = list(
        pl.pallas_call(
            functools.partial(attend_kernel, sets, roles, len(laid), start, final),
            out_shape=shapes,
            in_specs=[pl.BlockSpec(memory_space=pltpu.SMEM)] + [whole] * (1 + len(given)),
            out_specs=[whole] * len(shapes),
            scratch_shapes=scratch,
            compiler_params=VMEM,
            cost_estimate=pl.CostEstimate(flops=8 * pairs * HEAD_DIM, bytes_accessed=2**20, transcendentals=pairs),
            name=name,
        )(classes, segments, *given)
    )
    if laid_out:
        laid = (roles, *results[-2:])
    if start:
        splits = [results[count], splits[1]]
    return splits, results[:count], laid, results[0] if final else None


def shards(queries, key_rows, value_rows, span_place, span_offset, segment_number, block_class):
    vmem, hbm = pl.BlockSpec(memory_space=pltpu.VMEM), pl.BlockSpec(memory_space=pl.ANY)
    payload, tables, q_other = pl.pallas_call(
        keys_kernel,
        out_shape=[
            jax.ShapeDtypeStruct((SHARDS, 2 * ROWS, HEAD_DIM), jnp.bfloat16),
            jax.ShapeDtypeStruct((3, ROWS, HEAD_DIM), jnp.float32),
            jax.ShapeDtypeStruct((HEAD_DIM, WIDTH), jnp.bfloat16),
        ],
        in_specs=[hbm, hbm, vmem, hbm, hbm, hbm],
        out_specs=[vmem, vmem, vmem],
        scratch_shapes=[
            pltpu.VMEM((1, ROWS), jnp.int32),
            pltpu.VMEM((1, ROWS), jnp.int32),
            pltpu.VMEM((ROWS, 2 * HEAD_DIM), jnp.bfloat16),
            pltpu.VMEM((ROWS, 2 * HEAD_DIM), jnp.bfloat16),
            pltpu.VMEM((ROWS, WIDTH), jnp.bfloat16),
            pltpu.SemaphoreType.DMA((5,)),
        ],
        compiler_params=pltpu.CompilerParams(vmem_limit_bytes=KEYS_VMEM),
        name="rotate_keys",
    )(span_place[None, :], span_offset[None, :], lane_frequencies(), key_rows, value_rows, queries)
    own = lax.all_to_all(payload, "uly", split_axis=0, concat_axis=0, tiled=True)

    every = [(b, u) for b in range(BLOCKS) for u in range(SHARDS)]
    partners = [(b * SHARDS + u, b * SHARDS + partner_of(b, u)) for b, u in every]
    q_partner = lax.ppermute(q_other, ("blk", "uly"), partners)
    split_own, odds, segments = pl.pallas_call(
        own_queries_kernel,
        out_shape=[
            jax.ShapeDtypeStruct((2 * HEAD_DIM, WIDTH), jnp.bfloat16),
            jax.ShapeDtypeStruct((5 * BLOCK, ROWS), jnp.bfloat16),
            jax.ShapeDtypeStruct((5 * SHARDS, 1, ROWS), jnp.int32),
        ],
        in_specs=[vmem, vmem, hbm],
        out_specs=[vmem, vmem, vmem],
        scratch_shapes=[pltpu.SemaphoreType.DMA],
        compiler_params=VMEM,
        name="rotate_own_queries",
    )(queries, tables, segment_number.reshape(BLOCKS * SHARDS, 1, ROWS))
    own, split_own, odds, segments = lax.optimization_barrier((own, split_own, odds, segments))

    within = range(BLOCKS)
    ahead = [(i + 2 - 4 * (i % 2), i) for i in within if i + 2 - 4 * (i % 2) in within]
    behind = [(i - 2 + 4 * (i % 2), i) for i in within if i - 2 + 4 * (i % 2) in within]
    cores = [(i, i ^ 1) for i in within]
    far = lax.ppermute(own, "blk", ahead)
    back = lax.ppermute(own, "blk", behind)
    near = lax.ppermute(own, "blk", cores)

    run = functools.partial(attend, classes=block_class, segments=segments, odds=odds)
    both = (True, False)
    splits, state, _, _ = run("attend_own", sets=both, splits=(q_partner, split_own), blocks={"own": own})
    far, state = lax.optimization_barrier((far, state))
    late = lax.ppermute(far, "blk", cores)
    theirs = functools.partial(run, sets=both[:1], splits=splits[:1])
    _, passed, laid, _ = theirs("attend_near", state=state[:1], blocks={"near": near, "far": far})
    _, _, rest, to_send = theirs("attend_partner", state=passed, blocks={"late": late, "back": back}, final=True)
    others = lax.ppermute(to_send, ("blk", "uly"), partners)
    mine = run("attend_rest", sets=both[1:], splits=splits[1:], state=state[1:], laid=(laid, rest), final=True)[3]
    return pl.pallas_call(
        combine_kernel,
        out_shape=jax.ShapeDtypeStruct((ROWS, 2 * WIDTH), jnp.bfloat16),
        in_specs=[vmem, vmem],
        out_specs=hbm,
        scratch_shapes=[pltpu.SemaphoreType.DMA((2,))],
        compiler_params=VMEM,
        name="combine",
    )(mine, others)


def solution(mesh):
    rows = P(("blk", "uly"), None)
    line = P(("blk", "uly"))
    return jax.shard_map(
        shards,
        mesh=mesh,
        in_specs=(rows, rows, rows, line, line, P(), P()),
        out_specs=rows,
        check_vma=False,
    )
```

```python
import functools

import jax
import jax.numpy as jnp
import numpy as np
from jax import lax
from jax.experimental import pallas as pl
from jax.experimental.pallas import tpu as pltpu
from jax.sharding import PartitionSpec as P

HEAD_DIM = 128
HEADS_PER_GROUP = 8
WIDTH = HEADS_PER_GROUP * HEAD_DIM
ROWS = 128
SHARDS = 8
BLOCK = ROWS * SHARDS
BLOCKS = 64
STACK = 8
NEGATIVE = -1e30
SCALE = HEAD_DIM**-0.5 * 1.4426950408889634
MAXIMUM = HEAD_DIM + 8
VMEM = pltpu.CompilerParams(vmem_limit_bytes=16 * 2**20)
KEYS_VMEM = 60 * 2**20


def lane_frequencies():
    one = 10000.0 ** (-np.arange(16, dtype=np.float64) / 16)
    return np.concatenate([one, one, one, one, np.zeros(64)]).astype(np.float32)[None, :]


def partner_of(block, uly):
    return uly ^ (2 + 4 * (block % 2))


def rotate(x, cosine, minus, plus):
    return (
        x * cosine
        + pltpu.roll(x, HEAD_DIM - 16, axis=1) * minus
        + pltpu.roll(x, 16, axis=1) * plus
    )


def keys_kernel(*refs):
    place_in, offset_in, frequency, keys_in, values_in, queries_in = refs[:6]
    payload, tables, other, place, offset, keys, values, queries, staged, sems = refs[6:]
    group = 1 - lax.axis_index("uly") // 2 % 2
    queries_in = queries_in.at[:, pl.ds(pl.multiple_of(group * WIDTH, WIDTH), WIDTH)]
    pairs = (place_in, place), (offset_in, offset), (keys_in, keys), (values_in, values), (queries_in, queries)
    copies = [pltpu.make_async_copy(source, target, sems.at[i]) for i, (source, target) in enumerate(pairs)]
    for copy in copies:
        copy.start()
    copies[0].wait()
    copies[1].wait()
    shape = (ROWS, HEAD_DIM)
    lane = lax.broadcasted_iota(jnp.int32, shape, 1)
    by_place = jnp.broadcast_to(place[...].astype(jnp.float32), shape).T
    by_offset = jnp.broadcast_to(offset[...].astype(jnp.float32), shape).T
    angle = jnp.where(lane < 32, by_place, by_offset) * frequency[...]
    cosine, sine = jnp.cos(angle), jnp.sin(angle)
    first = lane % 32 < 16
    minus = jnp.where(first, -sine, 0.0)
    plus = jnp.where(first, 0.0, sine)
    tables[0], tables[1], tables[2] = cosine, minus, plus
    copies[2].wait()
    copies[3].wait()
    sent = []
    for group in range(2):
        lanes = slice(group * HEAD_DIM, (group + 1) * HEAD_DIM)
        turned = rotate(keys[:, lanes].astype(jnp.float32), cosine, minus, plus)
        staged[group, :ROWS, :] = turned.astype(jnp.bfloat16)
        staged[group, ROWS:, :] = values[:, lanes].astype(jnp.float32).T.astype(jnp.bfloat16)
        for peer in (2 * group, 2 * group + 1, 2 * group + 4, 2 * group + 5):
            sent.append(pltpu.make_async_copy(staged.at[group], payload.at[peer], sems.at[5 + len(sent)]))
            sent[-1].start()
    copies[4].wait()
    for head in range(HEADS_PER_GROUP):
        cols = slice(head * ROWS, (head + 1) * ROWS)
        turned = rotate(queries[:, cols].astype(jnp.float32), cosine, minus, plus).astype(jnp.bfloat16)
        other[:, cols] = turned.astype(jnp.float32).T.astype(jnp.bfloat16)
    for copy in sent:
        copy.wait()


def split_queries(x, odd, tip):
    x = x * SCALE
    high = x.astype(jnp.bfloat16)
    guard = jnp.where(tip == HEAD_DIM - 1, NEGATIVE, jnp.where(odd > 0.5, 0.0, NEGATIVE))
    low = jnp.where(tip < HEAD_DIM - 2, x - high.astype(jnp.float32), guard)
    return high, low.astype(jnp.bfloat16)


def turn_queries(queries, tables, group, head):
    start = pl.multiple_of(group * WIDTH + head * HEAD_DIM, HEAD_DIM)
    x = queries[:, pl.ds(start, HEAD_DIM)].astype(jnp.float32)
    return rotate(x, tables[0], tables[1], tables[2]).astype(jnp.bfloat16).astype(jnp.float32).T


def own_queries_kernel(queries, tables, all_segments, own, odds, segments, sem):
    me, uly = lax.axis_index("blk"), lax.axis_index("uly")
    square = (ROWS, ROWS)
    tip = lax.broadcasted_iota(jnp.int32, square, 0)
    base = jnp.clip(me - 2, 0, BLOCKS - 5)
    copy = pltpu.make_async_copy(all_segments.at[pl.ds(base * SHARDS, 5 * SHARDS)], segments, sem)
    copy.start()
    copy.wait()
    odd = jnp.broadcast_to((segments[(me - base) * SHARDS + uly] & 1).astype(jnp.float32), square)
    for head in range(HEADS_PER_GROUP):
        cols = slice(head * ROWS, (head + 1) * ROWS)
        high, low = split_queries(turn_queries(queries, tables, uly // 2 % 2, head), odd, tip)
        own[:HEAD_DIM, cols] = high
        own[HEAD_DIM:, cols] = low

    def chunk_step(c, carry):
        start = pl.multiple_of(c * ROWS, ROWS)
        column = jnp.broadcast_to((segments[c] & 1).astype(jnp.float32), square).T
        odds[pl.ds(start, ROWS), :] = column.astype(jnp.bfloat16)
        return carry

    lax.fori_loop(0, 5 * SHARDS, chunk_step, 0, unroll=4)


def attend_kernel(sets, roles, pairs, start, final, *refs):
    refs = list(refs)
    classes, segments, odds = refs.pop(0), refs.pop(0), refs.pop(0)
    count = len(sets)
    laid = [(refs.pop(0), refs.pop(0)) for _ in range(pairs)]
    if start:
        arrived = refs.pop(0)
        splits = [None, refs.pop(0)]
    else:
        splits = [refs.pop(0) for _ in range(count)]
    blocks = [] if pairs else [refs.pop(0) for _ in roles]
    given = [] if start else [refs.pop(0) for _ in range(count)]
    bias = refs.pop(-1) if start else None
    outs = [refs.pop(0) for _ in range(count)] if final else []
    if final:
        states = refs[-count:]
    else:
        states = [refs.pop(0) for _ in range(count)]
    if start:
        splits[0] = refs.pop(0)
    if not pairs:
        laid = [(refs.pop(0), refs.pop(0))]
    keys = [pair[0].at[i] for pair in laid for i in range(pair[0].shape[0])]
    values = [pair[1].at[i] for pair in laid for i in range(pair[1].shape[0])]

    me, uly = lax.axis_index("blk"), lax.axis_index("uly")
    step = 1 - 2 * (me % 2)
    distance_of = {"own": 0, "near": step, "far": 2 * step, "late": -step, "back": -2 * step}
    klass = classes[me]
    base = jnp.clip(me - 2, 0, BLOCKS - 5)
    square = (ROWS, ROWS)
    lane = lax.broadcasted_iota(jnp.int32, square, 1)
    tip = lax.broadcasted_iota(jnp.int32, square, 0)
    chunks = [partner_of(me, uly) if theirs else uly for theirs in sets]

    def odd_tokens(s, shape):
        segment = segments[(me - base) * SHARDS + chunks[s]]
        return jnp.broadcast_to((segment & 1).astype(jnp.float32), shape)

    def hidden(s, first, number):
        shape = (number, ROWS)
        at = pl.multiple_of((me - base) * BLOCK + first, ROWS)
        context = (odds[pl.ds(at, number), :].astype(jnp.float32) < 0.5) & (klass == 2)
        follows = (odd_tokens(s, shape) > 0.5) | (klass != 2)
        key_at = first + lax.broadcasted_iota(jnp.int32, shape, 0)
        token_at = chunks[s] * ROWS + lax.broadcasted_iota(jnp.int32, shape, 1)
        return jnp.where(context | (follows & (key_at <= token_at)), 0.0, NEGATIVE)

    facts = []
    for role in roles:
        distance = distance_of[role]
        there = me + distance
        seen = (there >= 0) & (there < BLOCKS) & ((klass != 1) | (distance <= 0))
        facts.append((distance, there, seen))

    def lay_out(j):
        distance, there, _ = facts[j]
        before = jnp.where((klass == 2) & (distance < 0), 1.0, 0.0)
        after = jnp.where((klass == 2) & (distance > 0), 1.0, 0.0)
        guard = jnp.where(lane == HEAD_DIM - 2, before, jnp.where(lane == HEAD_DIM - 1, after, 0.0))
        place = jnp.clip(there - base, 0, 4) * SHARDS
        for c in range(SHARDS):
            rows = slice(c * ROWS, (c + 1) * ROWS)
            part = blocks[j][c, :ROWS, :]
            keys[j][rows, :HEAD_DIM] = part
            odd = odds[pl.ds(pl.multiple_of((place + c) * ROWS, ROWS), ROWS), :].astype(jnp.float32)
            part = jnp.where(lane < HEAD_DIM - 2, part.astype(jnp.float32), odd * guard)
            keys[j][rows, HEAD_DIM:] = part.astype(jnp.bfloat16)
            values[j][:, rows] = blocks[j][c, ROWS:, :]

    wide = STACK * ROWS
    items = [
        (s, slice(tile * wide, (tile + 1) * wide)) for s in range(count) for tile in range(HEADS_PER_GROUP // STACK)
    ]

    def scores(j, s, cols):
        return jnp.dot(keys[j][...], splits[s][:, cols], preferred_element_type=jnp.float32)

    def take(which, masked):
        steps = [(j, s, cols) for j in which for s, cols in items]
        tops = [states[s][MAXIMUM : MAXIMUM + 1, :] for s in range(count)]
        ahead = scores(*steps[0])
        for i, (j, s, cols) in enumerate(steps):
            now, ahead = ahead, scores(*steps[i + 1]) if i + 1 < len(steps) else None
            if masked:
                now = now + jnp.concatenate([bias[s]] * STACK, axis=1)
            weights = jnp.exp2(now - tops[s][:, cols])
            part = jnp.dot(values[j][...], weights.astype(jnp.bfloat16), preferred_element_type=jnp.float32)
            states[s][:HEAD_DIM, cols] += part
            states[s][HEAD_DIM : HEAD_DIM + 1, cols] += jnp.sum(weights, axis=0, keepdims=True)

    def take_largest(which, masked):
        def head_step(head, carry):
            cols = pl.ds(pl.multiple_of(head * ROWS, ROWS), ROWS)
            for s in range(count):
                now = scores(which[0], s, cols)
                if masked:
                    now = now + bias[s]
                old = states[s][MAXIMUM : MAXIMUM + 1, cols]
                new = jnp.maximum(old, jnp.max(now, axis=0, keepdims=True))
                decay = jnp.exp2(old - new)
                weights = jnp.exp2(now - new)
                part = jnp.dot(values[which[0]][...], weights.astype(jnp.bfloat16), preferred_element_type=jnp.float32)
                states[s][:HEAD_DIM, cols] = states[s][:HEAD_DIM, cols] * decay + part
                total = states[s][HEAD_DIM : HEAD_DIM + 1, cols] * decay + jnp.sum(weights, axis=0, keepdims=True)
                states[s][HEAD_DIM : HEAD_DIM + 1, cols] = total
                states[s][MAXIMUM : MAXIMUM + 1, cols] = new
            return carry

        lax.fori_loop(0, HEADS_PER_GROUP, head_step, 0)

    def each_block(how):
        for j in range(len(roles)):

            @pl.when(facts[j][2])
            def _(j=j):
                how([j], False)

    def own_block(how):
        @pl.when(klass == 0)
        def _():
            how([0], False)

        @pl.when(klass != 0)
        def _():
            how([0], True)

    if start:
        odd = odd_tokens(0, square)
        for head in range(HEADS_PER_GROUP):
            cols = slice(head * ROWS, (head + 1) * ROWS)
            high, low = split_queries(arrived[:, cols].astype(jnp.float32), odd, tip)
            splits[0][:HEAD_DIM, cols] = high
            splits[0][HEAD_DIM:, cols] = low
        lay_out(0)
        for s in range(count):
            rows = pl.ds(pl.multiple_of(chunks[s] * ROWS, ROWS), ROWS)
            near = jnp.dot(keys[0][rows, :], splits[s][...], preferred_element_type=jnp.float32)
            near = near + jnp.concatenate([hidden(s, chunks[s] * ROWS, ROWS)] * HEADS_PER_GROUP, axis=1)
            states[s][:MAXIMUM, :] = jnp.zeros((MAXIMUM, WIDTH), jnp.float32)
            states[s][MAXIMUM : MAXIMUM + 1, :] = jnp.max(near, axis=0, keepdims=True)

        @pl.when(klass != 0)
        def _():
            for s in range(count):
                bias[s] = hidden(s, 0, BLOCK)

        own_block(take)
    else:
        for j in range(len(blocks)):
            lay_out(j)
        for s in range(count):
            states[s][...] = given[s][...]
        every = facts[0][2]
        for fact in facts[1:]:
            every = every & fact[2]

        @pl.when(every)
        def _():
            take(list(range(len(roles))), False)

        @pl.when(jnp.logical_not(every))
        def _():
            each_block(take)

    largest = states[0][HEAD_DIM : HEAD_DIM + 1, :]
    for s in range(1, count):
        largest = jnp.maximum(largest, states[s][HEAD_DIM : HEAD_DIM + 1, :])

    @pl.when(jnp.logical_not(jnp.max(largest) < 2.0**100))
    def _():
        for s in range(count):
            if start:
                states[s][:MAXIMUM, :] = jnp.zeros((MAXIMUM, WIDTH), jnp.float32)
            else:
                states[s][...] = given[s][...]
        if start:
            own_block(take_largest)
        else:
            each_block(take_largest)

    for s, out in enumerate(outs):
        share = 1.0 / states[s][HEAD_DIM : HEAD_DIM + 1, :]
        for head in range(HEADS_PER_GROUP):
            cols = slice(head * ROWS, (head + 1) * ROWS)
            out[:, cols] = (states[s][:HEAD_DIM, cols] * share[:, cols]).T.astype(jnp.bfloat16)


def combine_kernel(mine, others, out, sems):
    group = lax.axis_index("uly") // 2 % 2
    copies = [
        pltpu.make_async_copy(source, out.at[:, pl.ds(pl.multiple_of(which * WIDTH, WIDTH), WIDTH)], sems.at[i])
        for i, (source, which) in enumerate(((mine, group), (others, 1 - group)))
    ]
    for copy in copies:
        copy.start()
    for copy in copies:
        copy.wait()


def attend(name, classes, segments, odds, sets, splits, blocks=None, laid=(), state=None, final=False):
    roles = tuple(blocks) if blocks else tuple(role for group in laid for role in group[0])
    count, number = len(sets), len(roles)
    start = state is None
    whole = pl.BlockSpec(memory_space=pltpu.VMEM)
    state_shape, split_shape = (MAXIMUM + 8, WIDTH), (2 * HEAD_DIM, WIDTH)
    laid_shapes = [(number, BLOCK, 2 * HEAD_DIM), (number, HEAD_DIM, BLOCK)]
    shapes, scratch = [], []
    if final:
        shapes.append(jax.ShapeDtypeStruct((ROWS, WIDTH), jnp.bfloat16))
        laid_out = [jax.ShapeDtypeStruct(shape, jnp.bfloat16) for shape in laid_shapes] if blocks else []
        scratch += [pltpu.VMEM(state_shape, jnp.float32)] * count
    else:
        shapes += [jax.ShapeDtypeStruct(state_shape, jnp.float32)] * count
        laid_out = [jax.ShapeDtypeStruct(shape, jnp.bfloat16) for shape in laid_shapes] if blocks else []
        if start:
            scratch += [pltpu.VMEM(shape, jnp.bfloat16) for shape in laid_shapes]
            laid_out = []
            shapes.append(jax.ShapeDtypeStruct(split_shape, jnp.bfloat16))
            scratch.append(pltpu.VMEM((count, BLOCK, ROWS), jnp.float32))
    shapes += laid_out
    given = [odds, *(x for group in laid for x in group[1:]), *splits, *(blocks or {}).values(), *(state or ())]
    pairs = count * number * HEADS_PER_GROUP * ROWS * BLOCK
    results = list(
        pl.pallas_call(
            functools.partial(attend_kernel, sets, roles, len(laid), start, final),
            out_shape=shapes,
            in_specs=[pl.BlockSpec(memory_space=pltpu.SMEM)] + [whole] * (1 + len(given)),
            out_specs=[whole] * len(shapes),
            scratch_shapes=scratch,
            compiler_params=VMEM,
            cost_estimate=pl.CostEstimate(flops=8 * pairs * HEAD_DIM, bytes_accessed=2**20, transcendentals=pairs),
            name=name,
        )(classes, segments, *given)
    )
    if laid_out:
        laid = (roles, *results[-2:])
    if start:
        splits = [results[count], splits[1]]
    return splits, results[:count], laid, results[0] if final else None


def shards(queries, key_rows, value_rows, span_place, span_offset, segment_number, block_class):
    vmem, hbm = pl.BlockSpec(memory_space=pltpu.VMEM), pl.BlockSpec(memory_space=pl.ANY)
    payload, tables, q_other = pl.pallas_call(
        keys_kernel,
        out_shape=[
            jax.ShapeDtypeStruct((SHARDS, 2 * ROWS, HEAD_DIM), jnp.bfloat16),
            jax.ShapeDtypeStruct((3, ROWS, HEAD_DIM), jnp.float32),
            jax.ShapeDtypeStruct((HEAD_DIM, WIDTH), jnp.bfloat16),
        ],
        in_specs=[hbm, hbm, vmem, hbm, hbm, hbm],
        out_specs=[hbm, vmem, vmem],
        scratch_shapes=[
            pltpu.VMEM((1, ROWS), jnp.int32),
            pltpu.VMEM((1, ROWS), jnp.int32),
            pltpu.VMEM((ROWS, 2 * HEAD_DIM), jnp.bfloat16),
            pltpu.VMEM((ROWS, 2 * HEAD_DIM), jnp.bfloat16),
            pltpu.VMEM((ROWS, WIDTH), jnp.bfloat16),
            pltpu.VMEM((2, 2 * ROWS, HEAD_DIM), jnp.bfloat16),
            pltpu.SemaphoreType.DMA((13,)),
        ],
        compiler_params=pltpu.CompilerParams(vmem_limit_bytes=KEYS_VMEM),
        name="rotate_keys",
    )(span_place[None, :], span_offset[None, :], lane_frequencies(), key_rows, value_rows, queries)
    own = lax.all_to_all(payload, "uly", split_axis=0, concat_axis=0, tiled=True)

    every = [(b, u) for b in range(BLOCKS) for u in range(SHARDS)]
    partners = [(b * SHARDS + u, b * SHARDS + partner_of(b, u)) for b, u in every]
    q_partner = lax.ppermute(q_other, ("blk", "uly"), partners)
    split_own, odds, segments = pl.pallas_call(
        own_queries_kernel,
        out_shape=[
            jax.ShapeDtypeStruct((2 * HEAD_DIM, WIDTH), jnp.bfloat16),
            jax.ShapeDtypeStruct((5 * BLOCK, ROWS), jnp.bfloat16),
            jax.ShapeDtypeStruct((5 * SHARDS, 1, ROWS), jnp.int32),
        ],
        in_specs=[vmem, vmem, hbm],
        out_specs=[vmem, vmem, vmem],
        scratch_shapes=[pltpu.SemaphoreType.DMA],
        compiler_params=VMEM,
        name="rotate_own_queries",
    )(queries, tables, segment_number.reshape(BLOCKS * SHARDS, 1, ROWS))
    ready = (own, split_own, q_partner, odds, segments)
    own, split_own, q_partner, odds, segments = lax.optimization_barrier(ready)

    within = range(BLOCKS)
    ahead = [(i + 2 - 4 * (i % 2), i) for i in within if i + 2 - 4 * (i % 2) in within]
    behind = [(i - 2 + 4 * (i % 2), i) for i in within if i - 2 + 4 * (i % 2) in within]
    cores = [(i, i ^ 1) for i in within]
    far = lax.ppermute(own, "blk", ahead)
    back = lax.ppermute(own, "blk", behind)
    near = lax.ppermute(own, "blk", cores)

    run = functools.partial(attend, classes=block_class, segments=segments, odds=odds)
    both = (True, False)
    splits, state, _, _ = run("attend_own", sets=both, splits=(q_partner, split_own), blocks={"own": own})
    far, state = lax.optimization_barrier((far, state))
    late = lax.ppermute(far, "blk", cores)
    theirs = functools.partial(run, sets=both[:1], splits=splits[:1])
    _, passed, laid, _ = theirs("attend_near", state=state[:1], blocks={"near": near, "far": far})
    _, _, rest, to_send = theirs("attend_partner", state=passed, blocks={"late": late, "back": back}, final=True)
    others = lax.ppermute(to_send, ("blk", "uly"), partners)
    mine = run("attend_rest", sets=both[1:], splits=splits[1:], state=state[1:], laid=(laid, rest), final=True)[3]
    return pl.pallas_call(
        combine_kernel,
        out_shape=jax.ShapeDtypeStruct((ROWS, 2 * WIDTH), jnp.bfloat16),
        in_specs=[vmem, vmem],
        out_specs=hbm,
        scratch_shapes=[pltpu.SemaphoreType.DMA((2,))],
        compiler_params=VMEM,
        name="combine",
    )(mine, others)


def solution(mesh):
    rows = P(("blk", "uly"), None)
    line = P(("blk", "uly"))
    return jax.shard_map(
        shards,
        mesh=mesh,
        in_specs=(rows, rows, rows, line, line, P(), P()),
        out_specs=rows,
        check_vma=False,
    )
```
